32 devices in a mesh: parts: 2 (over x), clus: 16 (over z, y, core).
Axes of the slice: x: 2, y: 2, z: 4, core: 2. Of those that a mesh axis runs over, the one named last changes fastest.
Arguments:
- embeddings: float32 [65536, 768], P(('parts', 'clus')), parts along dimension 0, may hold values from -6 to 6
- coverage: bfloat16 [65536], P(('parts', 'clus')), parts along dimension 0, may hold values from 0.0019989014 to 0.059814453
- cluster_ids: int32 [65536, 1], P(('parts', 'clus')), parts along dimension 0, may hold values from 0 to 63, as said below
Outputs:
- gains: float32 [65536], P(('parts', 'clus')), parts along dimension 0
The draws below stay inside these ranges and needn't reach their ends.
There are 2 independent parts, one for each index of `parts`. The reference program is written for one: setup_inputs(seed, part) draws one part's arguments, and reference() takes and returns one part's arrays. A program takes and returns all parts, laid end to end along the dimension named above; each array names one. Nothing has to cross between parts.
Inputs may be any that keep to these rules, and one draw needn't show every extreme that they name: `cluster_ids`: cluster k belongs to owner k // 4. Among the 2048 documents of one device (aligned blocks of 2048 rows) no cluster appears more than 64 times and some cluster exactly 64 times; half of the owners receive exactly 192 of these documents and the other half exactly one third of 192.
All inputs are finite; a program needn't handle non-finite values.
Results may differ from the reference program's by a relative error of at most 0.00045.
Values may be sent and summed in bfloat16 or wider, within the bound.
No kernel may reach another device: no remote copies, remote signals or barrier semaphores. Data moves between devices by JAX's collectives and lax.ppermute only.
A program may use at most 128 MiB of HBM per device.

```python
import math
import jax
import jax.numpy as jnp
from jax import lax

D = 768
ROWS = 2048
CL_DEV = 4
CAP = 64
TOTAL = 32768
N_CLUS = 16


def draw_cluster_ids(key, part):
    key = jax.random.fold_in(key, 5)
    devices = TOTAL // ROWS
    quarter = ROWS // (4 * devices)

    def one_block(block_key):
        keys = jax.random.split(block_key, 5)
        heavy = jax.random.permutation(keys[0], devices) < devices // 2
        first = jax.random.randint(keys[1], (devices,), 0, 2 * quarter + 1)
        second = jax.random.randint(keys[2], (devices,), 0, 2 * quarter + 1)
        full_share = jnp.full((devices,), 2 * quarter, jnp.int32)
        nothing = jnp.zeros((devices,), jnp.int32)
        heavy_counts = jnp.stack([full_share, full_share, first, 2 * quarter - first], axis=1)
        light_counts = jnp.stack([second, 2 * quarter - second, nothing, nothing], axis=1)
        counts = jnp.where(heavy[:, None], heavy_counts, light_counts).astype(jnp.int32)
        owner_keys = jax.random.split(keys[3], devices)
        shuffles = jax.vmap(lambda k: jax.random.permutation(k, 4))(owner_keys)
        counts = jnp.take_along_axis(counts, shuffles, axis=1).reshape(-1)
        labels = jnp.repeat(jnp.arange(devices * 4, dtype=jnp.int32), counts, total_repeat_length=ROWS)
        return jax.random.permutation(keys[4], labels)
    blocks = jax.vmap(one_block)(jax.random.split(key, devices))
    return blocks.reshape(-1, 1).astype(jnp.int32)


def shard_levels(stream_key, shape, pieces, smallest, largest):
    loudness, own = 1.0, jax.random.fold_in(stream_key, 6)
    for dim, shards_of in pieces:
        draws = jnp.exp(jax.random.uniform(jax.random.fold_in(own, dim), (shards_of,), jnp.float32, smallest / len(pieces), largest / len(pieces)))
        loudness = loudness * jnp.repeat(draws, shape[dim] // shards_of).reshape([-1 if axis == dim else 1 for axis in range(len(shape))])
    return loudness


def gaussian(stream_key, shape, deviation, most, shards=(), kind=jnp.bfloat16):
    array = jax.random.normal(stream_key, shape, jnp.float32) * deviation
    if len(shards) > 0:
        array = shard_levels(stream_key, shape, shards, -0.22, 0.18) * array
    return jnp.clip(array, min=-most, max=most).astype(kind)


def setup_inputs(seed: int = 0, part: int = 0) -> dict:
    splits = jax.random.split(jax.random.key(seed), 4)
    part_keys = jax.random.split(jax.random.fold_in(splits[3], part), 4)
    embeddings = gaussian(part_keys[0], (TOTAL, D), 1.0, 6.0, ((0, 16),), jnp.float32)
    coverage = jnp.clip(jnp.exp(math.log(0.059814453) - 3.3986496 * jax.random.uniform(part_keys[1], (TOTAL,), jnp.float32) ** shard_levels(part_keys[1], (TOTAL,), ((0, 16),), -0.2, 0.2)), 0.0019989014, 0.059814453).astype(jnp.bfloat16)
    cluster_ids = draw_cluster_ids(jax.random.fold_in(jax.random.fold_in(splits[3], part), 71), part)
    return dict(embeddings=embeddings, coverage=coverage, cluster_ids=cluster_ids)


def reference(embeddings, coverage, cluster_ids):
    clusters = CL_DEV * N_CLUS
    width = N_CLUS * CAP
    total = embeddings.shape[0]
    sums = lax.optimization_barrier(jnp.sum(embeddings * embeddings, axis=1, keepdims=True))
    unit = (embeddings * lax.rsqrt(sums + 1e-06)).astype(jnp.bfloat16)
    ident = cluster_ids[:, 0]
    order = jnp.argsort(ident, stable=True).astype(jnp.int32)
    sorted_ids = jnp.concatenate([ident[order], jnp.full((width,), -1, jnp.int32)])
    sorted_unit = jnp.concatenate([unit[order].astype(jnp.float32), jnp.zeros((width, unit.shape[1]), jnp.float32)])
    sorted_cover = jnp.concatenate([coverage[order].astype(jnp.float32), jnp.zeros((width,), jnp.float32)])
    offsets = jnp.searchsorted(ident[order], jnp.arange(clusters, dtype=jnp.int32)).astype(jnp.int32)

    def one_cluster(pair):
        cluster, start = pair
        valid = lax.dynamic_slice_in_dim(sorted_ids, start, width, 0) == cluster
        members = jnp.where(valid[:, None], lax.dynamic_slice_in_dim(sorted_unit, start, width, 0), 0.0)
        cover = jnp.where(valid, lax.dynamic_slice_in_dim(sorted_cover, start, width, 0), 0.0)
        similar = jnp.dot(members, members.T, precision=lax.Precision.HIGHEST, preferred_element_type=jnp.float32)
        result = lax.optimization_barrier(jnp.sum(jnp.maximum(similar - cover[:, None], 0.0), axis=0))
        return jnp.where(valid, result, 0.0)
    per_cluster = lax.map(one_cluster, (jnp.arange(clusters, dtype=jnp.int32), offsets))
    positions = (offsets[:, None] + jnp.arange(width, dtype=jnp.int32)[None, :]).reshape(-1)
    placed = jnp.zeros((total + width,), jnp.float32).at[positions].add(per_cluster.reshape(-1))
    return jnp.zeros((total,), jnp.float32).at[order].set(placed[:total])
```

```python
import jax
import jax.numpy as jnp
from jax import lax
from jax.experimental import pallas as pl
from jax.experimental.pallas import tpu as pltpu
from jax.sharding import PartitionSpec as P

CL_DEV = 4
PARTS = 3
VMEM = 56 * 1024 * 1024

NN = (((1,), (0,)), ((), ()))
NT = (((1,), (1,)), ((), ()))


def dot(left, right, dims, precision=None):
    return lax.dot_general(
        left, right, dims, precision=precision, preferred_element_type=jnp.float32
    )


def lanes(n):
    return -(-n // 128) * 128


def hot(values, count, first=0):
    index = lax.broadcasted_iota(jnp.int32, (count, values.shape[1]), 0) + first
    return jnp.where(index == values, 1.0, 0.0).astype(jnp.bfloat16)


def place(ids, devices, cap):
    rows = ids.shape[1]
    clusters = CL_DEV * devices
    step = 256
    onehot = hot(ids, clusters)
    before = (
        lax.broadcasted_iota(jnp.int32, (step, step), 0)
        < lax.broadcasted_iota(jnp.int32, (step, step), 1)
    )
    before = jnp.where(before, 1.0, 0.0).astype(jnp.bfloat16)
    count = jnp.zeros((clusters, 1), jnp.float32)
    ranks = []
    for start in range(0, rows, step):
        piece = onehot[:, start : start + step]
        wide = piece.astype(jnp.float32)
        ahead = dot(piece, before, NN) + count
        ranks.append(ahead)
        count = count + jnp.sum(wide, axis=1, keepdims=True)
    k = lax.broadcasted_iota(jnp.int32, (clusters, clusters), 0)
    m = lax.broadcasted_iota(jnp.int32, (clusters, clusters), 1)
    j = k % CL_DEV
    plus = (j == 1) & (m == k - 1)
    minus = ((j == 2) & ((m == k) | (m == k + 1))) | ((j == 3) & (m == k))
    mix = (jnp.where(plus, 1.0, 0.0) - jnp.where(minus, 1.0, 0.0)).astype(jnp.bfloat16)
    wide_count = jnp.broadcast_to(count, (clusters, 128)).astype(jnp.bfloat16)
    base = dot(mix, wide_count, NN)[:, :1]
    jcol = lax.broadcasted_iota(jnp.int32, (clusters, 1), 0) % CL_DEV
    base = base + jnp.where(jcol >= 2, float(PARTS * cap), 0.0)
    position = []
    for i, start in enumerate(range(0, rows, step)):
        wide = onehot[:, start : start + step].astype(jnp.float32)
        position.append(jnp.sum(wide * (ranks[i] + base), axis=0, keepdims=True))
    position = jnp.concatenate(position, axis=1).astype(jnp.int32)
    return ids // CL_DEV, position


def first_kernel(devices, cap, block):
    def kernel(ids_ref, cover_ref, emb_ref, unit_ref, where_ref, meta_ref, out_ref, acc_ref):
        step = pl.program_id(0)
        last = pl.num_programs(0) - 1
        slots = devices * cap
        seg = lanes(PARTS * cap)

        @pl.when(step == 0)
        def _():
            ids = ids_ref[...]
            owner, position = place(ids, devices, cap)
            chunk = position // cap
            slot = chunk * slots + owner * cap + position - chunk * cap
            where_ref[0:1, :] = slot
            where_ref[1:2, :] = owner
            where_ref[2:3, :] = position
            own = hot(owner, devices)
            there = hot(position, seg)
            cover = own * cover_ref[...].astype(jnp.bfloat16)
            which = own * (ids % CL_DEV).astype(jnp.float32).astype(jnp.bfloat16)
            meta_ref[:, 0, :seg] = dot(cover, there, NT)
            meta_ref[:, 0, seg:] = dot(which, there, NT)
            acc_ref[...] = jnp.zeros_like(acc_ref)

        raw = emb_ref[...]
        sums = jnp.sum(raw * raw, axis=-1, keepdims=True)
        unit = (raw * lax.rsqrt(sums + 1e-06)).astype(jnp.bfloat16)
        begin = pl.multiple_of(step * block, block)
        unit_ref[pl.ds(begin, block), :] = unit
        slot = where_ref[0:1, pl.ds(begin, block)]
        acc_ref[...] += dot(hot(slot, slots), unit, NN)

        @pl.when(step == last)
        def _():
            out_ref[...] = acc_ref[...].astype(jnp.bfloat16)

    return kernel


def dispatch_kernel(slots, part, tile):
    def kernel(where_ref, unit_ref, out_ref):
        begin = pl.program_id(0) * tile
        pick = hot(where_ref[0:1, :], tile, part * slots + begin)
        out_ref[...] = dot(pick, unit_ref[...], NN).astype(jnp.bfloat16)

    return kernel


def column(row):
    return jnp.transpose(jnp.broadcast_to(row, (128, row.shape[1])))


def wide(col, n):
    return jnp.concatenate([col] * (n // 128), axis=1)


def pair(left_ref, right_ref, left_meta, right_meta, tile, both):
    rows = left_ref.shape[0]
    cols = right_ref.shape[0]
    cover_left = column(left_meta[0:1, :])
    which_left = column(left_meta[1:2, :])
    right = right_ref[...]
    down = jnp.zeros((8, cols), jnp.float32)
    across = []
    for start in range(0, rows, tile):
        similar = dot(left_ref[start : start + tile, :], right, NT)
        same = wide(which_left[start : start + tile], cols) == right_meta[1:2, :]
        similar = jnp.where(same, similar, -1e30)
        gain = jnp.maximum(similar - wide(cover_left[start : start + tile], cols), 0.0)
        down = down + jnp.sum(gain.reshape(tile // 8, 8, cols), axis=0)
        if both:
            other = jnp.maximum(similar - right_meta[0:1, :], 0.0)
            part = other[:, :128]
            for lane in range(128, cols, 128):
                part = part + other[:, lane : lane + 128]
            across.append(part)
    down = jnp.sum(down, axis=0, keepdims=True)
    if not both:
        return down, None
    across = jnp.concatenate(across, axis=0)
    across = jnp.sum(jnp.transpose(across), axis=0, keepdims=True)
    return down, across


def gram_first(tile):
    def kernel(meta_ref, a_ref, out_ref):
        down, _ = pair(a_ref, a_ref, meta_ref, meta_ref, tile, False)
        out_ref[...] = down

    return kernel


def gram_second(tile):
    def kernel(ma_ref, mb_ref, a_ref, b_ref, ga_ref, outa_ref, outb_ref):
        down, across = pair(a_ref, b_ref, ma_ref, mb_ref, tile, True)
        own, _ = pair(b_ref, b_ref, mb_ref, mb_ref, tile, False)
        outa_ref[...] = ga_ref[...] + across
        outb_ref[...] = down + own

    return kernel


def gram_third(tile, devices, cap):
    def kernel(mb_ref, mc_ref, b_ref, c_ref, ga_ref, gb_ref, out_ref):
        down, across = pair(b_ref, c_ref, mb_ref, mc_ref, tile, True)
        own, _ = pair(c_ref, c_ref, mc_ref, mc_ref, tile, False)
        all_gains = [ga_ref[...], gb_ref[...] + across, down + own]
        fill = jnp.zeros((1, out_ref.shape[2] - PARTS * cap), jnp.float32)
        for o in range(devices):
            parts = [g[:, o * cap : (o + 1) * cap] for g in all_gains]
            if fill.shape[1]:
                parts.append(fill)
            out_ref[o] = jnp.concatenate(parts, axis=1)

    return kernel


def last_kernel(devices):
    def kernel(where_ref, gains_ref, out_ref):
        gains = gains_ref[:, 0, :]
        high = gains.astype(jnp.bfloat16)
        rest = gains - high.astype(jnp.float32)
        mid = rest.astype(jnp.bfloat16)
        low = (rest - mid.astype(jnp.float32)).astype(jnp.bfloat16)
        there = hot(where_ref[2:3, :], gains.shape[1])
        found = dot(high, there, NN) + dot(mid, there, NN) + dot(low, there, NN)
        index = lax.broadcasted_iota(jnp.int32, found.shape, 0)
        mine = jnp.where(index == where_ref[1:2, :], found, 0.0)
        out_ref[...] = jnp.sum(mine, axis=0, keepdims=True)

    return kernel


def call(kernel, outs, cost, name, **extra):
    return pl.pallas_call(
        kernel,
        out_shape=outs,
        compiler_params=pltpu.CompilerParams(vmem_limit_bytes=VMEM),
        cost_estimate=pl.CostEstimate(flops=cost[0], bytes_accessed=cost[1], transcendentals=0),
        name=name,
        **extra,
    )


def body(embeddings, coverage, cluster_ids):
    devices = lax.axis_size("clus")
    rows, width = embeddings.shape
    clusters = CL_DEV * devices
    cap = 2 * rows // clusters
    slots = devices * cap
    seg = lanes(PARTS * cap)
    f32, bf16 = jnp.float32, jnp.bfloat16
    S = jax.ShapeDtypeStruct
    ids = cluster_ids.reshape(1, rows)
    cover = coverage.astype(f32).reshape(1, rows)
    block = rows // 4

    unit, where, meta, chunk_a = call(
        first_kernel(devices, cap, block),
        [S((rows, width), bf16), S((3, rows), jnp.int32), S((devices, 1, 2 * seg), f32), S((slots, width), bf16)],
        (2 * slots * rows * width, 4 * rows * width),
        "first",
        grid=(rows // block,),
        in_specs=[
            pl.BlockSpec((1, rows), lambda i: (0, 0)),
            pl.BlockSpec((1, rows), lambda i: (0, 0)),
            pl.BlockSpec((block, width), lambda i: (i, 0)),
        ],
        out_specs=[
            pl.BlockSpec((rows, width), lambda i: (0, 0)),
            pl.BlockSpec((3, rows), lambda i: (0, 0)),
            pl.BlockSpec((devices, 1, 2 * seg), lambda i: (0, 0, 0)),
            pl.BlockSpec((slots, width), lambda i: (0, 0)),
        ],
        scratch_shapes=[pltpu.VMEM((slots, width), f32)],
    )(ids, cover, embeddings)

    def swap(chunk):
        return lax.all_to_all(
            chunk.reshape(devices, cap, width), "clus", 0, 0, tiled=True
        ).reshape(slots, width)

    def dispatch(part):
        tile = slots // 2
        return call(
            dispatch_kernel(slots, part, tile),
            S((slots, width), bf16),
            (2 * slots * rows * width, 2 * rows * width),
            "dispatch",
            grid=(slots // tile,),
            in_specs=[
                pl.BlockSpec((3, rows), lambda i: (0, 0)),
                pl.BlockSpec((rows, width), lambda i: (0, 0)),
            ],
            out_specs=pl.BlockSpec((tile, width), lambda i: (i, 0)),
        )(where, unit)

    got_a = swap(chunk_a)
    met = lax.all_to_all(meta, "clus", 0, 0, tiled=True)
    got_b = swap(dispatch(1))
    got_c = swap(dispatch(2))

    met = met.reshape(devices, 2, seg)[:, :, : PARTS * cap].reshape(devices, 2, PARTS, cap)
    met = met.transpose(2, 1, 0, 3).reshape(PARTS, 2, slots)
    ma, mb, mc = met[0], met[1], met[2]

    square = 2 * slots * slots * width
    tile = slots // 4
    gain_a = call(gram_first(tile), S((1, slots), f32), (square, 2 * slots * width), "gram_a")(ma, got_a)
    gain_a, gain_b = call(
        gram_second(tile), [S((1, slots), f32)] * 2, (2 * square, 4 * slots * width), "gram_b"
    )(ma, mb, got_a, got_b, gain_a)
    gains = call(
        gram_third(tile, devices, cap), S((devices, 1, seg), f32), (2 * square, 4 * slots * width), "gram_c"
    )(mb, mc, got_b, got_c, gain_a, gain_b)
    back = lax.all_to_all(gains, "clus", 0, 0, tiled=True)
    out = call(last_kernel(devices), S((1, rows), f32), (2 * rows * seg * 48, 8 * rows), "last")(where, back)
    return out.reshape(rows)


def solution(mesh):
    placed = (P(("parts", "clus"), None), P(("parts", "clus")), P(("parts", "clus"), None))
    return jax.shard_map(
        body, mesh=mesh, in_specs=placed, out_specs=P(("parts", "clus")), check_vma=False
    )
```

```python
import jax
import jax.numpy as jnp
from jax import lax
from jax.experimental import pallas as pl
from jax.experimental.pallas import tpu as pltpu
from jax.sharding import PartitionSpec as P

CL_DEV = 4
PARTS = 3
EARLY = 3
MIB = 1024 * 1024

NN = (((1,), (0,)), ((), ()))
NT = (((1,), (1,)), ((), ()))


def dot(left, right, dims):
    return lax.dot_general(left, right, dims, preferred_element_type=jnp.float32)


def lanes(n):
    return -(-n // 128) * 128


def hot(values, count, first=0):
    index = lax.broadcasted_iota(jnp.int32, (count, values.shape[1]), 0) + first
    return jnp.where(index == values, 1.0, 0.0).astype(jnp.bfloat16)


def place(ids, devices, cap):
    rows = ids.shape[1]
    clusters = CL_DEV * devices
    step = 256
    onehot = hot(ids, clusters)
    before = lax.broadcasted_iota(jnp.int32, (step, step), 0) < lax.broadcasted_iota(
        jnp.int32, (step, step), 1
    )
    before = jnp.where(before, 1.0, 0.0).astype(jnp.bfloat16)
    count = jnp.zeros((clusters, 1), jnp.float32)
    ranks = []
    for start in range(0, rows, step):
        piece = onehot[:, start : start + step]
        ranks.append(dot(piece, before, NN) + count)
        count = count + jnp.sum(piece.astype(jnp.float32), axis=1, keepdims=True)
    k = lax.broadcasted_iota(jnp.int32, (clusters, clusters), 0)
    m = lax.broadcasted_iota(jnp.int32, (clusters, clusters), 1)
    j = k % CL_DEV
    plus = (j == 1) & (m == k - 1)
    minus = ((j == 2) & ((m == k) | (m == k + 1))) | ((j == 3) & (m == k))
    mix = (jnp.where(plus, 1.0, 0.0) - jnp.where(minus, 1.0, 0.0)).astype(jnp.bfloat16)
    spread = jnp.broadcast_to(count, (clusters, 128)).astype(jnp.bfloat16)
    base = dot(mix, spread, NN)[:, :1]
    jcol = lax.broadcasted_iota(jnp.int32, (clusters, 1), 0) % CL_DEV
    base = base + jnp.where(jcol >= 2, float(PARTS * cap), 0.0)
    position = []
    for i, start in enumerate(range(0, rows, step)):
        piece = onehot[:, start : start + step].astype(jnp.float32)
        position.append(jnp.sum(piece * (ranks[i] + base), axis=0, keepdims=True))
    return jnp.concatenate(position, axis=1).astype(jnp.int32)


def first_kernel(devices, cap, block, offsets):
    seg = PARTS * cap

    def kernel(ids_ref, emb_ref, unit_ref, where_ref, *rest):
        outs, acc_ref = rest[:-1], rest[-1]
        step = pl.program_id(0)
        last = pl.num_programs(0) - 1
        me = lax.axis_index("clus")

        @pl.when(step == 0)
        def _():
            ids = ids_ref[...]
            owner = ids // CL_DEV
            position = place(ids, devices, cap)
            where_ref[0:1, :] = owner * seg + position
            where_ref[1:2, :] = owner
            where_ref[2:3, :] = position
            where_ref[3:4, :] = ids - owner * CL_DEV
            acc_ref[...] = jnp.zeros_like(acc_ref)

        raw = emb_ref[...]
        sums = jnp.sum(raw * raw, axis=-1, keepdims=True)
        unit = (raw * lax.rsqrt(sums + 1e-06)).astype(jnp.bfloat16)
        begin = pl.multiple_of(step * block, block)
        unit_ref[pl.ds(begin, block), :] = unit
        code = where_ref[0:1, pl.ds(begin, block)]
        pick = jnp.concatenate([hot(code, seg, (me ^ k) * seg) for k in offsets], axis=0)
        acc_ref[...] += dot(pick, unit, NN)

        @pl.when(step == last)
        def _():
            for i, out_ref in enumerate(outs):
                out_ref[...] = acc_ref[i * seg : (i + 1) * seg, :].astype(jnp.bfloat16)

    return kernel


def rest_kernel(devices, cap, offsets):
    seg = PARTS * cap
    wide = lanes(seg)
    half = devices // 2

    def kernel(where_ref, cover_ref, unit_ref, meta_ref, near_ref, *outs):
        me = lax.axis_index("clus")
        own = hot(where_ref[1:2, :], devices)
        there = hot(where_ref[2:3, :], wide)
        cover = own * cover_ref[...].astype(jnp.bfloat16)
        which = own * where_ref[3:4, :].astype(jnp.float32).astype(jnp.bfloat16)
        meta_ref[:, 0, :wide] = dot(cover, there, NT)
        meta_ref[:, 0, wide:] = dot(which, there, NT)
        unit = unit_ref[...]
        code = where_ref[0:1, :]
        for k, out_ref in zip(offsets, outs):
            out_ref[...] = dot(hot(code, seg, (me ^ k) * seg), unit, NN).astype(jnp.bfloat16)
        first = (me // half) * half * seg
        size = half * seg
        tile = size // 4
        for start in range(0, size, tile):
            pick = hot(code, tile, first + start)
            near_ref[start : start + tile, :] = dot(pick, unit, NN).astype(jnp.bfloat16)

    return kernel


def column(row):
    return jnp.transpose(jnp.broadcast_to(row, (128, row.shape[1])))


def source(piece, me, half, offsets):
    if piece < half:
        return (me // half) * half + piece
    return me ^ offsets[piece - half]


def meta_kernel(devices, cap, offsets):
    seg = PARTS * cap
    wide = lanes(seg)
    half = devices // 2

    def kernel(met_ref, rows_ref, cover_ref, which_ref, zero_ref):
        me = lax.axis_index("clus")
        for p in range(devices):
            row = met_ref[source(p, me, half, offsets)]
            rows_ref[p] = row
            cover_ref[p * seg : (p + 1) * seg, :] = column(row[:, :wide])[:seg]
            which_ref[p * seg : (p + 1) * seg, :] = column(row[:, wide:])[:seg]
        zero_ref[...] = jnp.zeros_like(zero_ref)

    return kernel


def pad_rows(piece, count):
    if piece.shape[0] == count:
        return piece
    fill = jnp.zeros((count - piece.shape[0], piece.shape[1]), piece.dtype)
    return jnp.concatenate([piece, fill], axis=0)


def repeat(col, n):
    return jnp.concatenate([col] * (n // 128), axis=1)


def near_gram_kernel(devices, cap, tile):
    seg = PARTS * cap
    wide = lanes(seg)
    half = devices // 2
    group = max(1, 512 // wide)

    def kernel(rows_ref, cover_ref, which_ref, near_ref, gains_ref, out_ref):
        out_ref[...] = gains_ref[...]
        for p in range(0, half, group):
            members = range(p, p + group)
            right = jnp.concatenate(
                [pad_rows(near_ref[q * seg : (q + 1) * seg, :], wide) for q in members], axis=0
            )
            right_which = jnp.concatenate([rows_ref[q][:, wide:] for q in members], axis=1)
            down = jnp.zeros((8, group * wide), jnp.float32)
            for start in range(0, half * seg, tile):
                similar = dot(near_ref[start : start + tile, :], right, NT)
                n = group * wide
                same = repeat(which_ref[start : start + tile, :], n) == right_which
                gain = similar - repeat(cover_ref[start : start + tile, :], n)
                gain = jnp.where(same, jnp.maximum(gain, 0.0), 0.0)
                down = down + jnp.sum(gain.reshape(tile // 8, 8, n), axis=0)
            down = jnp.sum(down, axis=0, keepdims=True)
            for i, q in enumerate(members):
                out_ref[q] = out_ref[q] + down[:, i * wide : (i + 1) * wide]

    return kernel


def far_gram_kernel(devices, cap, offsets, done, new, final):
    seg = PARTS * cap
    wide = lanes(seg)
    half = devices // 2
    per_tile = max(1, 768 // seg)
    xs = list(range(half + done, half + new))

    def kernel(rows_ref, cover_ref, which_ref, near_ref, *rest):
        piece_refs, gains_ref, out_ref = rest[:-2], rest[-2], rest[-1]
        n = len(xs) * wide

        def rows_of(p):
            if p < half:
                return near_ref[p * seg : (p + 1) * seg, :]
            return piece_refs[p - half][...]

        right = jnp.concatenate([pad_rows(rows_of(p), wide) for p in xs], axis=0)
        right_cover = jnp.concatenate([rows_ref[p][:, :wide] for p in xs], axis=1)
        right_which = jnp.concatenate([rows_ref[p][:, wide:] for p in xs], axis=1)
        lane = lax.broadcasted_iota(jnp.int32, (1, wide), 1)
        inside = jnp.concatenate([lane < seg] * len(xs), axis=1)
        right_which = jnp.where(inside, right_which, -1.0)
        down = jnp.zeros((8, n), jnp.float32)
        total = {}
        order = list(range(half + done)) + xs
        for start in range(0, len(order), per_tile):
            members = order[start : start + per_tile]
            left = jnp.concatenate([rows_of(p) for p in members], axis=0)
            similar = dot(left, right, NT)
            low, high = members[0] * seg, (members[-1] + 1) * seg
            same = repeat(which_ref[low:high, :], n) == right_which
            similar = jnp.where(same, similar, -1e30)
            gain = jnp.maximum(similar - repeat(cover_ref[low:high, :], n), 0.0)
            down = down + jnp.sum(gain.reshape((high - low) // 8, 8, n), axis=0)
            old = [p for p in members if p < half + done]
            if not old:
                continue
            count = len(old) * seg
            other = jnp.maximum(similar[:count] - right_cover, 0.0)
            part = other[:, :128]
            for lane0 in range(128, n, 128):
                part = part + other[:, lane0 : lane0 + 128]
            for i, p in enumerate(old):
                mine = pad_rows(part[i * seg : (i + 1) * seg], wide)
                total[p] = jnp.sum(jnp.transpose(mine), axis=0, keepdims=True)
        down = jnp.sum(down, axis=0, keepdims=True)
        for i, p in enumerate(xs):
            total[p] = down[:, i * wide : (i + 1) * wide]
        me = lax.axis_index("clus")
        for p in range(devices):
            value = gains_ref[p]
            if p in total:
                value = value + total[p]
            if final:
                out_ref[source(p, me, half, offsets)] = value
            else:
                out_ref[p] = value

    return kernel


def last_kernel(kernel_devices):
    def kernel(where_ref, gains_ref, out_ref):
        gains = gains_ref[:, 0, :]
        high = gains.astype(jnp.bfloat16)
        rest = gains - high.astype(jnp.float32)
        mid = rest.astype(jnp.bfloat16)
        low = (rest - mid.astype(jnp.float32)).astype(jnp.bfloat16)
        there = hot(where_ref[2:3, :], gains.shape[1])
        found = dot(high, there, NN) + dot(mid, there, NN) + dot(low, there, NN)
        index = lax.broadcasted_iota(jnp.int32, found.shape, 0)
        mine = jnp.where(index == where_ref[1:2, :], found, 0.0)
        out_ref[...] = jnp.sum(mine, axis=0, keepdims=True)

    return kernel


def call(kernel, outs, cost, name, vmem=24, **extra):
    return pl.pallas_call(
        kernel,
        out_shape=outs,
        compiler_params=pltpu.CompilerParams(vmem_limit_bytes=vmem * MIB),
        cost_estimate=pl.CostEstimate(flops=cost[0], bytes_accessed=cost[1], transcendentals=0),
        name=name,
        **extra,
    )


def body(embeddings, coverage, cluster_ids):
    devices = lax.axis_size("clus")
    rows, width = embeddings.shape
    cap = 2 * rows // (CL_DEV * devices)
    seg = PARTS * cap
    wide = lanes(seg)
    half = devices // 2
    quarter = max(1, half // 2)
    offsets = []
    for i in range(quarter):
        offsets += [half + i, half + quarter + i]
    f32, bf16 = jnp.float32, jnp.bfloat16
    S = jax.ShapeDtypeStruct
    ids = cluster_ids.reshape(1, rows)
    cover = coverage.astype(f32).reshape(1, rows)
    block = rows // 4
    unitg = half // 8
    early = EARLY * unitg
    piece = S((seg, width), bf16)

    unit, where, *sent = call(
        first_kernel(devices, cap, block, offsets[:early]),
        [S((rows, width), bf16), S((4, rows), jnp.int32)] + [piece] * early,
        (2 * early * seg * rows * width, 4 * rows * width),
        "first",
        grid=(rows // block,),
        in_specs=[
            pl.BlockSpec((1, rows), lambda i: (0, 0)),
            pl.BlockSpec((block, width), lambda i: (i, 0)),
        ],
        out_specs=[
            pl.BlockSpec((rows, width), lambda i: (0, 0)),
            pl.BlockSpec((4, rows), lambda i: (0, 0)),
        ]
        + [pl.BlockSpec((seg, width), lambda i: (0, 0))] * early,
        scratch_shapes=[pltpu.VMEM((early * seg, width), f32)],
        vmem=56,
    )(ids, embeddings)
    meta, near, *others = call(
        rest_kernel(devices, cap, offsets[early:]),
        [S((devices, 1, 2 * wide), f32), S((half * seg, width), bf16)] + [piece] * (half - early),
        (0, 0),
        "rest",
    )(where, cover, unit)
    sent = sent + others

    far = []
    for i, x in enumerate(sent):
        if i >= early:
            x, far[i - early] = lax.optimization_barrier((x, far[i - early]))
        far.append(lax.ppermute(x, "clus", [(d, d ^ offsets[i]) for d in range(devices)]))
    meta, far[1] = lax.optimization_barrier((meta, far[1]))
    near, far[2] = lax.optimization_barrier((near, far[2]))
    met = lax.all_to_all(meta, "clus", 0, 0, tiled=True)
    groups = [[d for d in range(half)], [d for d in range(half, devices)]]
    near = lax.all_to_all(
        near.reshape(half, seg, width), "clus", 0, 0, tiled=True, axis_index_groups=groups
    ).reshape(half * seg, width)

    cols = S((devices * seg, 128), f32)
    gain_shape = S((devices, 1, wide), f32)
    row_meta, cover_col, which_col, gains = call(
        meta_kernel(devices, cap, offsets),
        [S((devices, 1, 2 * wide), f32), cols, cols, gain_shape],
        (0, 2 * devices * seg * 512),
        "meta",
    )(met)
    size = half * seg
    gains = call(
        near_gram_kernel(devices, cap, size // 2),
        gain_shape,
        (2 * size * size * width, 2 * size * width),
        "near_gram",
    )(row_meta, cover_col, which_col, near, gains)
    done = 0
    for new in [2 * unitg, 4 * unitg, 6 * unitg, 7 * unitg, 8 * unitg]:
        gains = call(
            far_gram_kernel(devices, cap, offsets, done, new, new == half),
            gain_shape,
            (2 * (half + new) * seg * (new - done) * seg * width, 2 * (half + new) * seg * width),
            "far_gram",
        )(row_meta, cover_col, which_col, near, *far[:new], gains)
        done = new
    back = lax.all_to_all(gains, "clus", 0, 0, tiled=True)
    out = call(last_kernel(devices), S((1, rows), f32), (2 * rows * wide * 48, 8 * rows), "last")(where, back)
    return out.reshape(rows)


def solution(mesh):
    placed = (P(("parts", "clus"), None), P(("parts", "clus")), P(("parts", "clus"), None))
    return jax.shard_map(
        body, mesh=mesh, in_specs=placed, out_specs=P(("parts", "clus")), check_vma=False
    )
```

```python
import jax
import jax.numpy as jnp
from jax import lax
from jax.experimental import pallas as pl
from jax.experimental.pallas import tpu as pltpu
from jax.sharding import PartitionSpec as P

CL_DEV = 4
PARTS = 3
EARLY = 3
DEPTH = 4
STOPS = (4, 6, 8, 10, 12, 14, 15, 16)
MIB = 1024 * 1024

NN = (((1,), (0,)), ((), ()))
NT = (((1,), (1,)), ((), ()))


def dot(left, right, dims):
    return lax.dot_general(left, right, dims, preferred_element_type=jnp.float32)


def lanes(n):
    return -(-n // 128) * 128


def hot(values, count, first=0):
    index = lax.broadcasted_iota(jnp.int32, (count, values.shape[1]), 0) + first
    return jnp.where(index == values, 1.0, 0.0).astype(jnp.bfloat16)


def place(ids, devices, cap):
    rows = ids.shape[1]
    clusters = CL_DEV * devices
    step = 256
    onehot = hot(ids, clusters)
    before = lax.broadcasted_iota(jnp.int32, (step, step), 0) < lax.broadcasted_iota(
        jnp.int32, (step, step), 1
    )
    before = jnp.where(before, 1.0, 0.0).astype(jnp.bfloat16)
    count = jnp.zeros((clusters, 1), jnp.float32)
    ranks = []
    for start in range(0, rows, step):
        piece = onehot[:, start : start + step]
        ranks.append(dot(piece, before, NN) + count)
        count = count + jnp.sum(piece.astype(jnp.float32), axis=1, keepdims=True)
    k = lax.broadcasted_iota(jnp.int32, (clusters, clusters), 0)
    m = lax.broadcasted_iota(jnp.int32, (clusters, clusters), 1)
    j = k % CL_DEV
    plus = (j == 1) & (m == k - 1)
    minus = ((j == 2) & ((m == k) | (m == k + 1))) | ((j == 3) & (m == k))
    mix = (jnp.where(plus, 1.0, 0.0) - jnp.where(minus, 1.0, 0.0)).astype(jnp.bfloat16)
    spread = jnp.broadcast_to(count, (clusters, 128)).astype(jnp.bfloat16)
    base = dot(mix, spread, NN)[:, :1]
    jcol = lax.broadcasted_iota(jnp.int32, (clusters, 1), 0) % CL_DEV
    base = base + jnp.where(jcol >= 2, float(PARTS * cap), 0.0)
    position = []
    for i, start in enumerate(range(0, rows, step)):
        piece = onehot[:, start : start + step].astype(jnp.float32)
        position.append(jnp.sum(piece * (ranks[i] + base), axis=0, keepdims=True))
    return jnp.concatenate(position, axis=1).astype(jnp.int32)


def first_kernel(devices, cap, block, offsets):
    seg = PARTS * cap

    def kernel(ids_ref, emb_ref, unit_ref, where_ref, *rest):
        outs, acc_ref = rest[:-1], rest[-1]
        step = pl.program_id(0)
        last = pl.num_programs(0) - 1
        me = lax.axis_index("clus")

        @pl.when(step == 0)
        def _():
            ids = ids_ref[...]
            owner = ids // CL_DEV
            position = place(ids, devices, cap)
            where_ref[0:1, :] = owner * seg + position
            where_ref[1:2, :] = owner
            where_ref[2:3, :] = position
            where_ref[3:4, :] = ids - owner * CL_DEV
            acc_ref[...] = jnp.zeros_like(acc_ref)

        raw = emb_ref[...]
        sums = jnp.sum(raw * raw, axis=-1, keepdims=True)
        unit = (raw * lax.rsqrt(sums + 1e-06)).astype(jnp.bfloat16)
        begin = pl.multiple_of(step * block, block)
        unit_ref[pl.ds(begin, block), :] = unit
        code = where_ref[0:1, pl.ds(begin, block)]
        pick = jnp.concatenate([hot(code, seg, (me ^ k) * seg) for k in offsets], axis=0)
        acc_ref[...] += dot(pick, unit, NN)

        @pl.when(step == last)
        def _():
            for i, out_ref in enumerate(outs):
                out_ref[...] = acc_ref[i * seg : (i + 1) * seg, :].astype(jnp.bfloat16)

    return kernel


def rest_kernel(devices, cap, offsets):
    seg = PARTS * cap
    wide = lanes(seg)

    def kernel(where_ref, cover_ref, unit_ref, meta_ref, *outs):
        me = lax.axis_index("clus")
        own = hot(where_ref[1:2, :], devices)
        there = hot(where_ref[2:3, :], wide)
        cover = own * cover_ref[...].astype(jnp.bfloat16)
        which = own * where_ref[3:4, :].astype(jnp.float32).astype(jnp.bfloat16)
        meta_ref[:, 0, :wide] = dot(cover, there, NT)
        meta_ref[:, 0, wide:] = dot(which, there, NT)
        unit = unit_ref[...]
        code = where_ref[0:1, :]
        for k, out_ref in zip(offsets, outs):
            out_ref[...] = dot(hot(code, seg, (me ^ k) * seg), unit, NN).astype(jnp.bfloat16)

    return kernel


def column(row):
    return jnp.transpose(jnp.broadcast_to(row, (128, row.shape[1])))


def meta_kernel(devices, cap, offsets):
    seg = PARTS * cap
    wide = lanes(seg)

    def kernel(met_ref, rows_ref, cover_ref, which_ref, zero_ref):
        me = lax.axis_index("clus")
        for p in range(devices):
            row = met_ref[me ^ offsets[p]]
            rows_ref[p] = row
            cover_ref[p * seg : (p + 1) * seg, :] = column(row[:, :wide])[:seg]
            which_ref[p * seg : (p + 1) * seg, :] = column(row[:, wide:])[:seg]
        zero_ref[...] = jnp.zeros_like(zero_ref)

    return kernel


def pad_rows(piece, count):
    if piece.shape[0] == count:
        return piece
    fill = jnp.zeros((count - piece.shape[0], piece.shape[1]), piece.dtype)
    return jnp.concatenate([piece, fill], axis=0)


def repeat(col, n):
    return jnp.concatenate([col] * (n // 128), axis=1)


def gram_kernel(devices, cap, offsets, done, new):
    seg = PARTS * cap
    wide = lanes(seg)
    per_tile = max(1, 768 // seg)
    xs = list(range(done, new))
    n = len(xs) * wide

    def kernel(rows_ref, cover_ref, which_ref, *rest):
        pieces, gains_ref, out_ref = rest[:-2], rest[-2], rest[-1]
        right = jnp.concatenate([pad_rows(pieces[p][...], wide) for p in xs], axis=0)
        right_cover = jnp.concatenate([rows_ref[p][:, :wide] for p in xs], axis=1)
        right_which = jnp.concatenate([rows_ref[p][:, wide:] for p in xs], axis=1)
        lane = lax.broadcasted_iota(jnp.int32, (1, wide), 1)
        inside = jnp.concatenate([lane < seg] * len(xs), axis=1)
        right_which = jnp.where(inside, right_which, -1.0)
        down = jnp.zeros((8, n), jnp.float32)
        total = {}
        for start in range(0, new, per_tile):
            members = range(start, min(start + per_tile, new))
            left = jnp.concatenate([pieces[p][...] for p in members], axis=0)
            similar = dot(left, right, NT)
            low, high = members[0] * seg, (members[-1] + 1) * seg
            same = repeat(which_ref[low:high, :], n) == right_which
            similar = jnp.where(same, similar, -1e30)
            gain = jnp.maximum(similar - repeat(cover_ref[low:high, :], n), 0.0)
            down = down + jnp.sum(gain.reshape((high - low) // 8, 8, n), axis=0)
            old = [p for p in members if p < done]
            if not old:
                continue
            count = len(old) * seg
            other = jnp.maximum(similar[:count] - right_cover, 0.0)
            part = other[:, :128]
            for begin in range(128, n, 128):
                part = part + other[:, begin : begin + 128]
            for i, p in enumerate(old):
                mine = pad_rows(part[i * seg : (i + 1) * seg], wide)
                total[p] = jnp.sum(jnp.transpose(mine), axis=0, keepdims=True)
        down = jnp.sum(down, axis=0, keepdims=True)
        for i, p in enumerate(xs):
            total[p] = down[:, i * wide : (i + 1) * wide]
        me = lax.axis_index("clus")
        for p in range(devices):
            value = gains_ref[p]
            if p in total:
                value = value + total[p]
            if new == devices:
                out_ref[me ^ offsets[p]] = value
            else:
                out_ref[p] = value

    return kernel


def last_kernel(kernel_devices):
    def kernel(where_ref, gains_ref, out_ref):
        gains = gains_ref[:, 0, :]
        high = gains.astype(jnp.bfloat16)
        rest = gains - high.astype(jnp.float32)
        mid = rest.astype(jnp.bfloat16)
        low = (rest - mid.astype(jnp.float32)).astype(jnp.bfloat16)
        there = hot(where_ref[2:3, :], gains.shape[1])
        found = dot(high, there, NN) + dot(mid, there, NN) + dot(low, there, NN)
        index = lax.broadcasted_iota(jnp.int32, found.shape, 0)
        mine = jnp.where(index == where_ref[1:2, :], found, 0.0)
        out_ref[...] = jnp.sum(mine, axis=0, keepdims=True)

    return kernel


def call(kernel, outs, cost, name, vmem=24, **extra):
    return pl.pallas_call(
        kernel,
        out_shape=outs,
        compiler_params=pltpu.CompilerParams(vmem_limit_bytes=vmem * MIB),
        cost_estimate=pl.CostEstimate(flops=cost[0], bytes_accessed=cost[1], transcendentals=0),
        name=name,
        **extra,
    )


def sequence(devices):
    half = devices // 2
    quarter = max(1, half // 2)
    far = []
    for i in range(quarter):
        far += [half + i, half + quarter + i]
    near = sorted(range(1, half), key=lambda k: (-k.bit_length(), k))
    order = [0, far[0]]
    for i in range(half - 2):
        order += [far[i + 1], near[i]]
    return order + [near[-1], far[-1]]


def body(embeddings, coverage, cluster_ids):
    devices = lax.axis_size("clus")
    rows, width = embeddings.shape
    cap = 2 * rows // (CL_DEV * devices)
    seg = PARTS * cap
    wide = lanes(seg)
    offsets = sequence(devices)
    f32, bf16 = jnp.float32, jnp.bfloat16
    S = jax.ShapeDtypeStruct
    ids = cluster_ids.reshape(1, rows)
    cover = coverage.astype(f32).reshape(1, rows)
    block = rows // 4
    unitg = devices // 16
    early = EARLY * unitg
    depth = DEPTH * unitg
    piece = S((seg, width), bf16)
    later = [0] + offsets[1 + early :]

    unit, where, *sent = call(
        first_kernel(devices, cap, block, offsets[1 : 1 + early]),
        [S((rows, width), bf16), S((4, rows), jnp.int32)] + [piece] * early,
        (2 * early * seg * rows * width, 4 * rows * width),
        "first",
        grid=(rows // block,),
        in_specs=[
            pl.BlockSpec((1, rows), lambda i: (0, 0)),
            pl.BlockSpec((block, width), lambda i: (i, 0)),
        ],
        out_specs=[
            pl.BlockSpec((rows, width), lambda i: (0, 0)),
            pl.BlockSpec((4, rows), lambda i: (0, 0)),
        ]
        + [pl.BlockSpec((seg, width), lambda i: (0, 0))] * early,
        scratch_shapes=[pltpu.VMEM((early * seg, width), f32)],
        vmem=56,
    )(ids, embeddings)
    meta, own, *others = call(
        rest_kernel(devices, cap, later),
        [S((devices, 1, 2 * wide), f32)] + [piece] * len(later),
        (0, 0),
        "rest",
        vmem=56,
    )(where, cover, unit)
    sent = sent + others

    got = []
    for i, x in enumerate(sent):
        if i >= depth:
            x, got[i - depth] = lax.optimization_barrier((x, got[i - depth]))
        got.append(lax.ppermute(x, "clus", [(d, d ^ offsets[1 + i]) for d in range(devices)]))
    meta, got[1] = lax.optimization_barrier((meta, got[1]))
    met = lax.all_to_all(meta, "clus", 0, 0, tiled=True)
    pieces = [own] + got

    cols = S((devices * seg, 128), f32)
    gain_shape = S((devices, 1, wide), f32)
    row_meta, cover_col, which_col, gains = call(
        meta_kernel(devices, cap, offsets),
        [S((devices, 1, 2 * wide), f32), cols, cols, gain_shape],
        (0, 2 * devices * seg * 512),
        "meta",
    )(met)
    done = 0
    for new in STOPS:
        new = new * unitg
        gains = call(
            gram_kernel(devices, cap, offsets, done, new),
            gain_shape,
            (2 * new * seg * (new - done) * seg * width, 2 * new * seg * width),
            "gram",
            vmem=16,
        )(row_meta, cover_col, which_col, *pieces[:new], gains)
        done = new
    back = lax.all_to_all(gains, "clus", 0, 0, tiled=True)
    out = call(last_kernel(devices), S((1, rows), f32), (2 * rows * wide * 48, 8 * rows), "last")(where, back)
    return out.reshape(rows)


def solution(mesh):
    placed = (P(("parts", "clus"), None), P(("parts", "clus")), P(("parts", "clus"), None))
    return jax.shard_map(
        body, mesh=mesh, in_specs=placed, out_specs=P(("parts", "clus")), check_vma=False
    )
```

```python
import jax
import jax.numpy as jnp
from jax import lax
from jax.experimental import pallas as pl
from jax.experimental.pallas import tpu as pltpu
from jax.sharding import PartitionSpec as P

CL_DEV = 4
PARTS = 3
EARLY = 1
DEPTH = 4
STOPS = (4, 6, 8, 10, 12, 14, 15, 16)
MIB = 1024 * 1024

NN = (((1,), (0,)), ((), ()))
NT = (((1,), (1,)), ((), ()))


def dot(left, right, dims):
    return lax.dot_general(left, right, dims, preferred_element_type=jnp.float32)


def lanes(n):
    return -(-n // 128) * 128


def hot(values, count, first=0):
    index = lax.broadcasted_iota(jnp.int32, (count, values.shape[1]), 0) + first
    return jnp.where(index == values, 1.0, 0.0).astype(jnp.bfloat16)


def place(ids, devices, cap):
    rows = ids.shape[1]
    clusters = CL_DEV * devices
    step = 256
    onehot = hot(ids, clusters)
    before = lax.broadcasted_iota(jnp.int32, (step, step), 0) < lax.broadcasted_iota(
        jnp.int32, (step, step), 1
    )
    before = jnp.where(before, 1.0, 0.0).astype(jnp.bfloat16)
    count = jnp.zeros((clusters, 1), jnp.float32)
    ranks = []
    for start in range(0, rows, step):
        piece = onehot[:, start : start + step]
        ranks.append(dot(piece, before, NN) + count)
        count = count + jnp.sum(piece.astype(jnp.float32), axis=1, keepdims=True)
    k = lax.broadcasted_iota(jnp.int32, (clusters, clusters), 0)
    m = lax.broadcasted_iota(jnp.int32, (clusters, clusters), 1)
    j = k % CL_DEV
    plus = (j == 1) & (m == k - 1)
    minus = ((j == 2) & ((m == k) | (m == k + 1))) | ((j == 3) & (m == k))
    mix = (jnp.where(plus, 1.0, 0.0) - jnp.where(minus, 1.0, 0.0)).astype(jnp.bfloat16)
    spread = jnp.broadcast_to(count, (clusters, 128)).astype(jnp.bfloat16)
    base = dot(mix, spread, NN)[:, :1]
    jcol = lax.broadcasted_iota(jnp.int32, (clusters, 1), 0) % CL_DEV
    base = base + jnp.where(jcol >= 2, float(PARTS * cap), 0.0)
    position = []
    for i, start in enumerate(range(0, rows, step)):
        piece = onehot[:, start : start + step].astype(jnp.float32)
        position.append(jnp.sum(piece * (ranks[i] + base), axis=0, keepdims=True))
    return jnp.concatenate(position, axis=1).astype(jnp.int32)


def first_kernel(devices, cap, steps, offsets):
    seg = PARTS * cap

    def kernel(ids_ref, emb_ref, unit_ref, where_ref, *rest):
        count = len(offsets)
        outs, scratch = rest[:count], rest[count:]
        raw_ref, rows_ref, piece_ref, in_sems, rows_sems, out_sems = scratch
        me = lax.axis_index("clus")
        block = raw_ref.shape[0] // steps

        def load(i):
            part = pl.ds(i * block, block)
            return pltpu.make_async_copy(emb_ref.at[part], raw_ref.at[part], in_sems.at[i])

        def store(i):
            part = pl.ds(i * block, block)
            return pltpu.make_async_copy(rows_ref.at[part], unit_ref.at[part], rows_sems.at[i])

        for i in range(steps):
            load(i).start()
        ids = ids_ref[...]
        owner = ids // CL_DEV
        position = place(ids, devices, cap)
        code = owner * seg + position
        where_ref[0:1, :] = code
        where_ref[1:2, :] = owner
        where_ref[2:3, :] = position
        where_ref[3:4, :] = ids - owner * CL_DEV
        for i in range(steps):
            load(i).wait()
            raw = raw_ref[i * block : (i + 1) * block, :]
            sums = jnp.sum(raw * raw, axis=-1, keepdims=True)
            unit = (raw * lax.rsqrt(sums + 1e-06)).astype(jnp.bfloat16)
            rows_ref[i * block : (i + 1) * block, :] = unit
            store(i).start()
        send_pieces(code, rows_ref, seg, me, offsets, outs, piece_ref, out_sems)
        for i in range(steps):
            store(i).wait()

    return kernel


def send_pieces(code, unit_ref, seg, me, offsets, outs, piece_ref, sems):
    copies = []
    for i, (k, out_ref) in enumerate(zip(offsets, outs)):
        pick = hot(code, seg, (me ^ k) * seg)
        piece_ref[i] = dot(pick, unit_ref[...], NN).astype(jnp.bfloat16)
        copies.append(pltpu.make_async_copy(piece_ref.at[i], out_ref, sems.at[i]))
        copies[-1].start()
    for copy in copies:
        copy.wait()


def second_kernel(devices, cap, offsets):
    seg = PARTS * cap
    wide = lanes(seg)

    def kernel(where_ref, cover_ref, unit_ref, meta_ref, *rest):
        outs, (piece_ref, sems) = rest[: len(offsets)], rest[len(offsets) :]
        me = lax.axis_index("clus")
        own = hot(where_ref[1:2, :], devices)
        there = hot(where_ref[2:3, :], wide)
        cover = own * cover_ref[...].astype(jnp.bfloat16)
        which = own * where_ref[3:4, :].astype(jnp.float32).astype(jnp.bfloat16)
        meta_ref[:, 0, :wide] = dot(cover, there, NT)
        meta_ref[:, 0, wide:] = dot(which, there, NT)
        send_pieces(where_ref[0:1, :], unit_ref, seg, me, offsets, outs, piece_ref, sems)

    return kernel


def rest_kernel(devices, cap, offsets):
    seg = PARTS * cap

    def kernel(where_ref, unit_ref, *rest):
        outs, (piece_ref, sems) = rest[: len(offsets)], rest[len(offsets) :]
        me = lax.axis_index("clus")
        send_pieces(where_ref[0:1, :], unit_ref, seg, me, offsets, outs, piece_ref, sems)

    return kernel


def column(row):
    return jnp.transpose(jnp.broadcast_to(row, (128, row.shape[1])))


def meta_kernel(devices, cap, offsets):
    seg = PARTS * cap
    wide = lanes(seg)

    def kernel(met_ref, rows_ref, cover_ref, which_ref, zero_ref):
        me = lax.axis_index("clus")
        for p in range(devices):
            row = met_ref[me ^ offsets[p]]
            rows_ref[p] = row
            cover_ref[p * seg : (p + 1) * seg, :] = column(row[:, :wide])[:seg]
            which_ref[p * seg : (p + 1) * seg, :] = column(row[:, wide:])[:seg]
        zero_ref[...] = jnp.zeros_like(zero_ref)

    return kernel


def pad_rows(piece, count):
    if piece.shape[0] == count:
        return piece
    fill = jnp.zeros((count - piece.shape[0], piece.shape[1]), piece.dtype)
    return jnp.concatenate([piece, fill], axis=0)


def repeat(col, n):
    return jnp.concatenate([col] * (n // 128), axis=1)


def gram_kernel(devices, cap, offsets, done, new):
    seg = PARTS * cap
    wide = lanes(seg)
    per_tile = max(1, 768 // seg)
    xs = list(range(done, new))
    n = len(xs) * wide

    def kernel(rows_ref, cover_ref, which_ref, *rest):
        pieces, gains_ref, out_ref = rest[:-2], rest[-2], rest[-1]
        right = jnp.concatenate([pad_rows(pieces[p][...], wide) for p in xs], axis=0)
        right_cover = jnp.concatenate([rows_ref[p][:, :wide] for p in xs], axis=1)
        right_which = jnp.concatenate([rows_ref[p][:, wide:] for p in xs], axis=1)
        lane = lax.broadcasted_iota(jnp.int32, (1, wide), 1)
        inside = jnp.concatenate([lane < seg] * len(xs), axis=1)
        right_which = jnp.where(inside, right_which, -1.0)
        down = jnp.zeros((8, n), jnp.float32)
        total = {}
        for start in range(0, new, per_tile):
            members = range(start, min(start + per_tile, new))
            left = jnp.concatenate([pieces[p][...] for p in members], axis=0)
            similar = dot(left, right, NT)
            low, high = members[0] * seg, (members[-1] + 1) * seg
            same = repeat(which_ref[low:high, :], n) == right_which
            similar = jnp.where(same, similar, -1e30)
            gain = jnp.maximum(similar - repeat(cover_ref[low:high, :], n), 0.0)
            down = down + jnp.sum(gain.reshape((high - low) // 8, 8, n), axis=0)
            old = [p for p in members if p < done]
            if not old:
                continue
            count = len(old) * seg
            other = jnp.maximum(similar[:count] - right_cover, 0.0)
            part = other[:, :128]
            for begin in range(128, n, 128):
                part = part + other[:, begin : begin + 128]
            for i, p in enumerate(old):
                mine = pad_rows(part[i * seg : (i + 1) * seg], wide)
                total[p] = jnp.sum(jnp.transpose(mine), axis=0, keepdims=True)
        down = jnp.sum(down, axis=0, keepdims=True)
        for i, p in enumerate(xs):
            total[p] = down[:, i * wide : (i + 1) * wide]
        me = lax.axis_index("clus")
        for p in range(devices):
            value = gains_ref[p]
            if p in total:
                value = value + total[p]
            if new == devices:
                out_ref[me ^ offsets[p]] = value
            else:
                out_ref[p] = value

    return kernel


def last_kernel(kernel_devices):
    def kernel(where_ref, gains_ref, out_ref):
        gains = gains_ref[:, 0, :]
        high = gains.astype(jnp.bfloat16)
        rest = gains - high.astype(jnp.float32)
        mid = rest.astype(jnp.bfloat16)
        low = (rest - mid.astype(jnp.float32)).astype(jnp.bfloat16)
        there = hot(where_ref[2:3, :], gains.shape[1])
        found = dot(high, there, NN) + dot(mid, there, NN) + dot(low, there, NN)
        index = lax.broadcasted_iota(jnp.int32, found.shape, 0)
        mine = jnp.where(index == where_ref[1:2, :], found, 0.0)
        out_ref[...] = jnp.sum(mine, axis=0, keepdims=True)

    return kernel


def call(kernel, outs, cost, name, vmem=24, **extra):
    return pl.pallas_call(
        kernel,
        out_shape=outs,
        compiler_params=pltpu.CompilerParams(vmem_limit_bytes=vmem * MIB),
        cost_estimate=pl.CostEstimate(flops=cost[0], bytes_accessed=cost[1], transcendentals=0),
        name=name,
        **extra,
    )


def sequence(devices):
    half = devices // 2
    quarter = max(1, half // 2)
    far = []
    for i in range(quarter):
        far += [half + i, half + quarter + i]
    near = sorted(range(1, half), key=lambda k: (-k.bit_length(), k))
    order = [0, far[0]]
    for i in range(half - 2):
        order += [far[i + 1], near[i]]
    return order + [near[-1], far[-1]]


def body(embeddings, coverage, cluster_ids):
    devices = lax.axis_size("clus")
    rows, width = embeddings.shape
    cap = 2 * rows // (CL_DEV * devices)
    seg = PARTS * cap
    wide = lanes(seg)
    offsets = sequence(devices)
    f32, bf16 = jnp.float32, jnp.bfloat16
    S = jax.ShapeDtypeStruct
    ids = cluster_ids.reshape(1, rows)
    cover = coverage.astype(f32).reshape(1, rows)
    unitg = devices // 16
    early = EARLY * unitg
    depth = DEPTH * unitg
    piece = S((seg, width), bf16)

    def pieces_of(count):
        return dict(
            out_specs=[pl.BlockSpec(memory_space=pltpu.HBM)] * count,
            scratch_shapes=[pltpu.VMEM((count, seg, width), bf16), pltpu.SemaphoreType.DMA((count,))],
        )

    full = pl.BlockSpec(memory_space=pltpu.VMEM)
    steps = 8
    lead = pieces_of(early)
    unit, where, *sent = call(
        first_kernel(devices, cap, steps, offsets[1 : 1 + early]),
        [S((rows, width), bf16), S((4, rows), jnp.int32)] + [piece] * early,
        (2 * early * seg * rows * width, 4 * rows * width),
        "first",
        in_specs=[full, pl.BlockSpec(memory_space=pltpu.HBM)],
        out_specs=[pl.BlockSpec(memory_space=pltpu.HBM), full] + lead["out_specs"],
        scratch_shapes=[pltpu.VMEM((rows, width), f32), pltpu.VMEM((rows, width), bf16)]
        + [lead["scratch_shapes"][0], pltpu.SemaphoreType.DMA((steps,))]
        + [pltpu.SemaphoreType.DMA((steps,)), lead["scratch_shapes"][1]],
        vmem=56,
    )(ids, embeddings)
    middle = pieces_of(depth - early)
    meta, *others = call(
        second_kernel(devices, cap, offsets[1 + early : 1 + depth]),
        [S((devices, 1, 2 * wide), f32)] + [piece] * (depth - early),
        (0, 0),
        "second",
        in_specs=[full] * 3,
        out_specs=[full] + middle["out_specs"],
        scratch_shapes=middle["scratch_shapes"],
        vmem=12,
    )(where, cover, unit)
    sent = sent + others
    met = lax.all_to_all(meta, "clus", 0, 0, tiled=True)
    after, met = lax.optimization_barrier((where, met))
    later = [0] + offsets[1 + depth :]
    own, *others = call(
        rest_kernel(devices, cap, later),
        [piece] * len(later),
        (0, 0),
        "rest",
        in_specs=[full] * 2,
        vmem=20,
        **pieces_of(len(later)),
    )(after, unit)
    sent = sent + others

    got = []
    for i, x in enumerate(sent):
        if i >= depth:
            x, got[i - depth] = lax.optimization_barrier((x, got[i - depth]))
        got.append(lax.ppermute(x, "clus", [(d, d ^ offsets[1 + i]) for d in range(devices)]))
    pieces = [own] + got

    cols = S((devices * seg, 128), f32)
    gain_shape = S((devices, 1, wide), f32)
    row_meta, cover_col, which_col, gains = call(
        meta_kernel(devices, cap, offsets),
        [S((devices, 1, 2 * wide), f32), cols, cols, gain_shape],
        (0, 2 * devices * seg * 512),
        "meta",
    )(met)
    done = 0
    for new in STOPS:
        new = new * unitg
        gains = call(
            gram_kernel(devices, cap, offsets, done, new),
            gain_shape,
            (2 * new * seg * (new - done) * seg * width, 2 * new * seg * width),
            "gram",
            vmem=16,
        )(row_meta, cover_col, which_col, *pieces[:new], gains)
        done = new
    back = lax.all_to_all(gains, "clus", 0, 0, tiled=True)
    out = call(last_kernel(devices), S((1, rows), f32), (2 * rows * wide * 48, 8 * rows), "last")(where, back)
    return out.reshape(rows)


def solution(mesh):
    placed = (P(("parts", "clus"), None), P(("parts", "clus")), P(("parts", "clus"), None))
    return jax.shard_map(
        body, mesh=mesh, in_specs=placed, out_specs=P(("parts", "clus")), check_vma=False
    )
```

```python
import jax
import jax.numpy as jnp
from jax import lax
from jax.experimental import pallas as pl
from jax.experimental.pallas import tpu as pltpu
from jax.sharding import PartitionSpec as P

CL_DEV = 4
PARTS = 3
TAIL = 16
EARLY = 1
DEPTH = 4
STOPS = (4, 6, 8, 10, 12, 14, 15, 16)
MIB = 1024 * 1024

NN = (((1,), (0,)), ((), ()))
NT = (((1,), (1,)), ((), ()))


def dot(left, right, dims):
    return lax.dot_general(left, right, dims, preferred_element_type=jnp.float32)


def lanes(n):
    return -(-n // 128) * 128


def hot(values, count, first=0):
    index = lax.broadcasted_iota(jnp.int32, (count, values.shape[1]), 0) + first
    return jnp.where(index == values, 1.0, 0.0).astype(jnp.bfloat16)


def place(ids, devices, cap):
    rows = ids.shape[1]
    clusters = CL_DEV * devices
    step = 256
    onehot = hot(ids, clusters)
    before = lax.broadcasted_iota(jnp.int32, (step, step), 0) < lax.broadcasted_iota(
        jnp.int32, (step, step), 1
    )
    before = jnp.where(before, 1.0, 0.0).astype(jnp.bfloat16)
    count = jnp.zeros((clusters, 1), jnp.float32)
    ranks = []
    for start in range(0, rows, step):
        piece = onehot[:, start : start + step]
        ranks.append(dot(piece, before, NN) + count)
        count = count + jnp.sum(piece.astype(jnp.float32), axis=1, keepdims=True)
    k = lax.broadcasted_iota(jnp.int32, (clusters, clusters), 0)
    m = lax.broadcasted_iota(jnp.int32, (clusters, clusters), 1)
    j = k % CL_DEV
    plus = (j == 1) & (m == k - 1)
    minus = ((j == 2) & ((m == k) | (m == k + 1))) | ((j == 3) & (m == k))
    mix = (jnp.where(plus, 1.0, 0.0) - jnp.where(minus, 1.0, 0.0)).astype(jnp.bfloat16)
    spread = jnp.broadcast_to(count, (clusters, 128)).astype(jnp.bfloat16)
    base = dot(mix, spread, NN)[:, :1]
    jcol = lax.broadcasted_iota(jnp.int32, (clusters, 1), 0) % CL_DEV
    base = base + jnp.where(jcol >= 2, float(PARTS * cap), 0.0)
    position = []
    for i, start in enumerate(range(0, rows, step)):
        piece = onehot[:, start : start + step].astype(jnp.float32)
        position.append(jnp.sum(piece * (ranks[i] + base), axis=0, keepdims=True))
    return jnp.concatenate(position, axis=1).astype(jnp.int32)


def first_kernel(devices, cap, steps, offsets):
    seg = PARTS * cap
    wide = lanes(seg)

    def kernel(ids_ref, cover_ref, emb_ref, unit_ref, where_ref, meta_ref, *rest):
        count = len(offsets)
        outs, scratch = rest[:count], rest[count:]
        raw_ref, rows_ref, piece_ref, in_sems, rows_sems, out_sems = scratch
        me = lax.axis_index("clus")
        block = raw_ref.shape[0] // steps

        def load(i):
            part = pl.ds(i * block, block)
            return pltpu.make_async_copy(emb_ref.at[part], raw_ref.at[part], in_sems.at[i])

        def store(i):
            part = pl.ds(i * block, block)
            return pltpu.make_async_copy(rows_ref.at[part], unit_ref.at[part], rows_sems.at[i])

        for i in range(steps):
            load(i).start()
        ids = ids_ref[...]
        owner = ids // CL_DEV
        position = place(ids, devices, cap)
        code = owner * seg + position
        where_ref[0:1, :] = code
        where_ref[1:2, :] = owner
        where_ref[2:3, :] = position
        own = hot(owner, devices)
        there = hot(position, wide)
        cover = cover_ref[...].astype(jnp.float32)
        cover = jnp.concatenate([cover[i : i + 1] for i in range(cover.shape[0])], axis=1)
        which = (ids - owner * CL_DEV).astype(jnp.float32)
        meta_ref[:, 0, :wide] = dot(own * cover.astype(jnp.bfloat16), there, NT)
        meta_ref[:, 0, wide:] = dot(own * which.astype(jnp.bfloat16), there, NT)
        for i in range(steps):
            load(i).wait()
            raw = raw_ref[i * block : (i + 1) * block, :]
            sums = jnp.sum(raw * raw, axis=-1, keepdims=True)
            unit = (raw * lax.rsqrt(sums + 1e-06)).astype(jnp.bfloat16)
            rows_ref[i * block : (i + 1) * block, :] = unit
            store(i).start()
        send_pieces(code, rows_ref, meta_ref, seg, me, offsets, outs, piece_ref, out_sems)
        for i in range(steps):
            store(i).wait()

    return kernel


def send_pieces(code, unit_ref, meta_ref, seg, me, offsets, outs, piece_ref, sems):
    copies = []
    slabs = unit_ref.shape[1] // 128
    index = lax.broadcasted_iota(jnp.int32, (TAIL, 128), 0)
    for i, (k, out_ref) in enumerate(zip(offsets, outs)):
        pick = hot(code, seg, (me ^ k) * seg)
        found = dot(pick, unit_ref[...], NN).astype(jnp.bfloat16)
        for f in range(slabs):
            piece_ref[i, f * seg : (f + 1) * seg, :] = found[:, f * 128 : (f + 1) * 128]
        row = meta_ref[me ^ k]
        tail = jnp.zeros((TAIL, 128), jnp.float32)
        for j in range(row.shape[1] // 128):
            tail = jnp.where(index == j, row[:, j * 128 : (j + 1) * 128], tail)
        piece_ref[i, slabs * seg :, :] = tail.astype(jnp.bfloat16)
        copies.append(pltpu.make_async_copy(piece_ref.at[i], out_ref, sems.at[i]))
        copies[-1].start()
    for copy in copies:
        copy.wait()


def rest_kernel(devices, cap, offsets):
    seg = PARTS * cap

    def kernel(where_ref, meta_ref, unit_ref, *rest):
        outs, (piece_ref, sems) = rest[: len(offsets)], rest[len(offsets) :]
        me = lax.axis_index("clus")
        send_pieces(where_ref[0:1, :], unit_ref, meta_ref, seg, me, offsets, outs, piece_ref, sems)

    return kernel


def column(row):
    return jnp.transpose(jnp.broadcast_to(row, (128, row.shape[1])))


def pad_rows(piece, count):
    if piece.shape[0] == count:
        return piece
    fill = jnp.zeros((count - piece.shape[0], piece.shape[1]), piece.dtype)
    return jnp.concatenate([piece, fill], axis=0)


def repeat(col, n):
    return jnp.concatenate([col] * (n // 128), axis=1)


def gram_kernel(devices, cap, offsets, stops, which_stop):
    seg = PARTS * cap
    wide = lanes(seg)
    per_tile = max(1, 768 // seg)
    done = stops[which_stop - 1] if which_stop else 0
    new = stops[which_stop]
    xs = list(range(done, new))
    n = len(xs) * wide
    final = new == devices

    def kernel(*refs):
        pieces, refs = refs[:new], refs[new:]
        old_cols, refs = refs[:which_stop], refs[which_stop:]
        if which_stop:
            gains_ref, refs = refs[0], refs[1:]
        out_ref = refs[0]
        slabs = (pieces[0].shape[0] - TAIL) // seg

        def rows_of(p):
            return jnp.concatenate([pieces[p][f * seg : (f + 1) * seg, :] for f in range(slabs)], axis=1)

        def meta_of(p):
            tail = pieces[p][slabs * seg :, :].astype(jnp.float32)
            parts = [tail[j : j + 1] for j in range(2 * wide // 128)]
            half = len(parts) // 2
            return jnp.concatenate(parts[:half], axis=1), jnp.concatenate(parts[half:], axis=1)

        metas = [meta_of(p) for p in xs]
        right = jnp.concatenate([pad_rows(rows_of(p), wide) for p in xs], axis=0)
        right_cover = jnp.concatenate([m[0] for m in metas], axis=1)
        right_which = jnp.concatenate([m[1] for m in metas], axis=1)
        lane = lax.broadcasted_iota(jnp.int32, (1, wide), 1)
        inside = jnp.concatenate([lane < seg] * len(xs), axis=1)
        right_which = jnp.where(inside, right_which, -1.0)
        cover_cols, which_cols = {}, {}
        first = 0
        for g in range(which_stop):
            for p in range(first, stops[g]):
                part = slice((p - first) * seg, (p - first + 1) * seg)
                cover_cols[p] = old_cols[g][part, :128]
                which_cols[p] = old_cols[g][part, 128:]
            first = stops[g]
        for i, p in enumerate(xs):
            cover_cols[p] = column(metas[i][0])[:seg]
            which_cols[p] = column(metas[i][1])[:seg]
            if not final:
                refs[1][i * seg : (i + 1) * seg, :128] = cover_cols[p]
                refs[1][i * seg : (i + 1) * seg, 128:] = which_cols[p]
        down = jnp.zeros((8, n), jnp.float32)
        total = {}
        for start in range(0, new, per_tile):
            members = range(start, min(start + per_tile, new))
            left = jnp.concatenate([rows_of(p) for p in members], axis=0)
            similar = dot(left, right, NT)
            count = len(members) * seg
            which = jnp.concatenate([which_cols[p] for p in members], axis=0)
            cover = jnp.concatenate([cover_cols[p] for p in members], axis=0)
            similar = jnp.where(repeat(which, n) == right_which, similar, -1e30)
            gain = jnp.maximum(similar - repeat(cover, n), 0.0)
            down = down + jnp.sum(gain.reshape(count // 8, 8, n), axis=0)
            old = [p for p in members if p < done]
            if not old:
                continue
            other = jnp.maximum(similar[: len(old) * seg] - right_cover, 0.0)
            part = other[:, :128]
            for begin in range(128, n, 128):
                part = part + other[:, begin : begin + 128]
            for i, p in enumerate(old):
                mine = pad_rows(part[i * seg : (i + 1) * seg], wide)
                total[p] = jnp.sum(jnp.transpose(mine), axis=0, keepdims=True)
        down = jnp.sum(down, axis=0, keepdims=True)
        for i, p in enumerate(xs):
            total[p] = down[:, i * wide : (i + 1) * wide]
        me = lax.axis_index("clus")
        for p in range(new):
            value = total[p]
            if p < done:
                value = value + gains_ref[p]
            if final:
                out_ref[me ^ offsets[p]] = value
            else:
                out_ref[p] = value

    return kernel


def last_kernel(kernel_devices):
    def kernel(where_ref, gains_ref, out_ref):
        gains = gains_ref[:, 0, :]
        high = gains.astype(jnp.bfloat16)
        rest = gains - high.astype(jnp.float32)
        mid = rest.astype(jnp.bfloat16)
        low = (rest - mid.astype(jnp.float32)).astype(jnp.bfloat16)
        there = hot(where_ref[2:3, :], gains.shape[1])
        found = dot(high, there, NN) + dot(mid, there, NN) + dot(low, there, NN)
        index = lax.broadcasted_iota(jnp.int32, found.shape, 0)
        mine = jnp.where(index == where_ref[1:2, :], found, 0.0)
        out_ref[...] = jnp.sum(mine, axis=0, keepdims=True)

    return kernel


def call(kernel, outs, cost, name, vmem=24, **extra):
    return pl.pallas_call(
        kernel,
        out_shape=outs,
        compiler_params=pltpu.CompilerParams(vmem_limit_bytes=vmem * MIB),
        cost_estimate=pl.CostEstimate(flops=cost[0], bytes_accessed=cost[1], transcendentals=0),
        name=name,
        **extra,
    )


def sequence(devices):
    half = devices // 2
    quarter = max(1, half // 2)
    far = []
    for i in range(quarter):
        far += [half + i, half + quarter + i]
    near = sorted(range(1, half), key=lambda k: (-k.bit_length(), k))
    order = [0, far[0]]
    for i in range(half - 2):
        order += [far[i + 1], near[i]]
    return order + [near[-1], far[-1]]


def body(embeddings, coverage, cluster_ids):
    devices = lax.axis_size("clus")
    rows, width = embeddings.shape
    cap = 2 * rows // (CL_DEV * devices)
    seg = PARTS * cap
    wide = lanes(seg)
    offsets = sequence(devices)
    f32, bf16 = jnp.float32, jnp.bfloat16
    S = jax.ShapeDtypeStruct
    ids = cluster_ids.reshape(1, rows)
    cover = coverage.reshape(rows // 128, 128)
    unitg = devices // 16
    early = EARLY * unitg
    depth = DEPTH * unitg
    tall = width // 128 * seg + TAIL
    piece = S((tall, 128), bf16)

    def pieces_of(count):
        return dict(
            out_specs=[pl.BlockSpec(memory_space=pltpu.HBM)] * count,
            scratch_shapes=[pltpu.VMEM((count, tall, 128), bf16), pltpu.SemaphoreType.DMA((count,))],
        )

    full = pl.BlockSpec(memory_space=pltpu.VMEM)
    hbm = pl.BlockSpec(memory_space=pltpu.HBM)
    steps = 8
    lead = pieces_of(early)
    unit, where, meta, *sent = call(
        first_kernel(devices, cap, steps, offsets[1 : 1 + early]),
        [S((rows, width), bf16), S((3, rows), jnp.int32), S((devices, 1, 2 * wide), f32)] + [piece] * early,
        (2 * early * seg * rows * width, 4 * rows * width),
        "first",
        in_specs=[full, full, hbm],
        out_specs=[hbm, full, full] + lead["out_specs"],
        scratch_shapes=[pltpu.VMEM((rows, width), f32), pltpu.VMEM((rows, width), bf16)]
        + [lead["scratch_shapes"][0], pltpu.SemaphoreType.DMA((steps,))]
        + [pltpu.SemaphoreType.DMA((steps,)), lead["scratch_shapes"][1]],
        vmem=56,
    )(ids, cover, embeddings)
    for name, ks in (("second", offsets[1 + early : 1 + depth]), ("rest", offsets[1 + depth :] + [0])):
        sent += call(
            rest_kernel(devices, cap, ks),
            [piece] * len(ks),
            (0, 0),
            name,
            in_specs=[full] * 3,
            vmem=20,
            **pieces_of(len(ks)),
        )(where, meta, unit)
    own = sent.pop()

    got = []
    for i, x in enumerate(sent):
        if i >= depth:
            x, got[i - depth] = lax.optimization_barrier((x, got[i - depth]))
        got.append(lax.ppermute(x, "clus", [(d, d ^ offsets[1 + i]) for d in range(devices)]))
    pieces = [own] + got

    gain_shape = S((devices, 1, wide), f32)
    stops = [stop * unitg for stop in STOPS]
    cols, gains = [], []
    for g, new in enumerate(stops):
        fresh = new - (stops[g - 1] if g else 0)
        gains, *more = call(
            gram_kernel(devices, cap, offsets, stops, g),
            [gain_shape] + [S((fresh * seg, 256), f32)] * (new < devices),
            (2 * new * seg * fresh * seg * width, 2 * new * seg * width),
            "gram",
            vmem=16,
        )(*pieces[:new], *cols, *([gains] if g else []))
        cols += more
    back = lax.all_to_all(gains, "clus", 0, 0, tiled=True)
    out = call(last_kernel(devices), S((1, rows), f32), (2 * rows * wide * 48, 8 * rows), "last")(where, back)
    return out.reshape(rows)


def solution(mesh):
    placed = (P(("parts", "clus"), None), P(("parts", "clus")), P(("parts", "clus"), None))
    return jax.shard_map(
        body, mesh=mesh, in_specs=placed, out_specs=P(("parts", "clus")), check_vma=False
    )
```

```python
import jax
import jax.numpy as jnp
from jax import lax
from jax.experimental import pallas as pl
from jax.experimental.pallas import tpu as pltpu
from jax.sharding import PartitionSpec as P

CL_DEV = 4
PARTS = 3
TAIL = 16
EARLY = 1
DEPTH = 4
STOPS = (4, 6, 8, 10, 12, 14, 15, 16)
MIB = 1024 * 1024

NN = (((1,), (0,)), ((), ()))
NT = (((1,), (1,)), ((), ()))


def dot(left, right, dims):
    return lax.dot_general(left, right, dims, preferred_element_type=jnp.float32)


def lanes(n):
    return -(-n // 128) * 128


def hot(values, count, first=0):
    index = lax.broadcasted_iota(jnp.int32, (count, values.shape[1]), 0) + first
    return jnp.where(index == values, 1.0, 0.0).astype(jnp.bfloat16)


def place(ids, devices, cap):
    rows = ids.shape[1]
    clusters = CL_DEV * devices
    step = 256
    onehot = hot(ids, clusters)
    before = lax.broadcasted_iota(jnp.int32, (step, step), 0) < lax.broadcasted_iota(
        jnp.int32, (step, step), 1
    )
    before = jnp.where(before, 1.0, 0.0).astype(jnp.bfloat16)
    count = jnp.zeros((clusters, 1), jnp.float32)
    ranks = []
    for start in range(0, rows, step):
        piece = onehot[:, start : start + step]
        ranks.append(dot(piece, before, NN) + count)
        count = count + jnp.sum(piece.astype(jnp.float32), axis=1, keepdims=True)
    k = lax.broadcasted_iota(jnp.int32, (clusters, clusters), 0)
    m = lax.broadcasted_iota(jnp.int32, (clusters, clusters), 1)
    j = k % CL_DEV
    plus = (j == 1) & (m == k - 1)
    minus = ((j == 2) & ((m == k) | (m == k + 1))) | ((j == 3) & (m == k))
    mix = (jnp.where(plus, 1.0, 0.0) - jnp.where(minus, 1.0, 0.0)).astype(jnp.bfloat16)
    spread = jnp.broadcast_to(count, (clusters, 128)).astype(jnp.bfloat16)
    base = dot(mix, spread, NN)[:, :1]
    jcol = lax.broadcasted_iota(jnp.int32, (clusters, 1), 0) % CL_DEV
    base = base + jnp.where(jcol >= 2, float(PARTS * cap), 0.0)
    position = []
    for i, start in enumerate(range(0, rows, step)):
        piece = onehot[:, start : start + step].astype(jnp.float32)
        position.append(jnp.sum(piece * (ranks[i] + base), axis=0, keepdims=True))
    return jnp.concatenate(position, axis=1).astype(jnp.int32)


def first_kernel(devices, cap, steps, offsets):
    seg = PARTS * cap
    wide = lanes(seg)

    def kernel(ids_hbm, cover_hbm, emb_ref, unit_ref, where_hbm, meta_hbm, *rest):
        count = len(offsets)
        outs, scratch = rest[:count], rest[count:]
        ids_ref, cover_ref, raw_ref, rows_ref, where_ref, meta_ref, piece_ref = scratch[:7]
        in_sems, rows_sems, out_sems, small_sems = scratch[7:]
        me = lax.axis_index("clus")
        block = raw_ref.shape[0] // steps

        def load(i):
            part = pl.ds(i * block, block)
            return pltpu.make_async_copy(emb_ref.at[part], raw_ref.at[part], in_sems.at[i])

        def store(i):
            part = pl.ds(i * block, block)
            return pltpu.make_async_copy(rows_ref.at[part], unit_ref.at[part], rows_sems.at[i])

        small = [
            pltpu.make_async_copy(ids_hbm, ids_ref, small_sems.at[0]),
            pltpu.make_async_copy(cover_hbm, cover_ref, small_sems.at[1]),
            pltpu.make_async_copy(where_ref, where_hbm, small_sems.at[2]),
            pltpu.make_async_copy(meta_ref, meta_hbm, small_sems.at[3]),
        ]
        small[0].start()
        small[1].start()
        for i in range(steps):
            load(i).start(priority=i % 2)
        small[0].wait()
        small[1].wait()
        ids = ids_ref[...]
        owner = ids // CL_DEV
        position = place(ids, devices, cap)
        code = owner * seg + position
        where_ref[0:1, :] = code
        where_ref[1:2, :] = owner
        where_ref[2:3, :] = position
        own = hot(owner, devices)
        there = hot(position, wide)
        cover = cover_ref[...].astype(jnp.float32)
        cover = jnp.concatenate([cover[i : i + 1] for i in range(cover.shape[0])], axis=1)
        which = (ids - owner * CL_DEV).astype(jnp.float32)
        meta_ref[:, 0, :wide] = dot(own * cover.astype(jnp.bfloat16), there, NT)
        meta_ref[:, 0, wide:] = dot(own * which.astype(jnp.bfloat16), there, NT)
        small[2].start()
        small[3].start()
        for i in range(steps):
            load(i).wait()
            if i == steps - 1:
                for before in range(steps - 1):
                    store(before).start(priority=before % 2)
            raw = raw_ref[i * block : (i + 1) * block, :]
            sums = jnp.sum(raw * raw, axis=-1, keepdims=True)
            unit = (raw * lax.rsqrt(sums + 1e-06)).astype(jnp.bfloat16)
            rows_ref[i * block : (i + 1) * block, :] = unit
        store(steps - 1).start()
        send_pieces(code, rows_ref, meta_ref, seg, me, offsets, outs, piece_ref, out_sems)
        small[2].wait()
        small[3].wait()
        for i in range(steps):
            store(i).wait()

    return kernel


def send_pieces(code, unit_ref, meta_ref, seg, me, offsets, outs, piece_ref, sems):
    copies = []
    slabs = unit_ref.shape[1] // 128
    index = lax.broadcasted_iota(jnp.int32, (TAIL, 128), 0)
    for i, (k, out_ref) in enumerate(zip(offsets, outs)):
        pick = hot(code, seg, (me ^ k) * seg)
        found = dot(pick, unit_ref[...], NN).astype(jnp.bfloat16)
        for f in range(slabs):
            piece_ref[i, f * seg : (f + 1) * seg, :] = found[:, f * 128 : (f + 1) * 128]
        row = meta_ref[me ^ k]
        tail = jnp.zeros((TAIL, 128), jnp.float32)
        for j in range(row.shape[1] // 128):
            tail = jnp.where(index == j, row[:, j * 128 : (j + 1) * 128], tail)
        piece_ref[i, slabs * seg :, :] = tail.astype(jnp.bfloat16)
        copies.append(pltpu.make_async_copy(piece_ref.at[i], out_ref, sems.at[i]))
        copies[-1].start()
    for copy in copies:
        copy.wait()


def rest_kernel(devices, cap, offsets):
    seg = PARTS * cap

    def kernel(where_ref, meta_ref, unit_ref, *rest):
        outs, (piece_ref, sems) = rest[: len(offsets)], rest[len(offsets) :]
        me = lax.axis_index("clus")
        send_pieces(where_ref[0:1, :], unit_ref, meta_ref, seg, me, offsets, outs, piece_ref, sems)

    return kernel


def column(row):
    return jnp.transpose(jnp.broadcast_to(row, (128, row.shape[1])))


def pad_rows(piece, count):
    if piece.shape[0] == count:
        return piece
    fill = jnp.zeros((count - piece.shape[0], piece.shape[1]), piece.dtype)
    return jnp.concatenate([piece, fill], axis=0)


def repeat(col, n):
    return jnp.concatenate([col] * (n // 128), axis=1)


def gram_kernel(devices, cap, offsets, stops, which_stop):
    seg = PARTS * cap
    wide = lanes(seg)
    per_tile = max(1, 768 // seg)
    done = stops[which_stop - 1] if which_stop else 0
    new = stops[which_stop]
    xs = list(range(done, new))
    n = len(xs) * wide
    final = new == devices

    def kernel(*refs):
        pieces, refs = refs[:new], refs[new:]
        old_cols, refs = refs[:which_stop], refs[which_stop:]
        if which_stop:
            gains_ref, refs = refs[0], refs[1:]
        out_ref = refs[0]
        slabs = (pieces[0].shape[0] - TAIL) // seg

        def rows_of(p):
            return jnp.concatenate([pieces[p][f * seg : (f + 1) * seg, :] for f in range(slabs)], axis=1)

        def meta_of(p):
            tail = pieces[p][slabs * seg :, :].astype(jnp.float32)
            parts = [tail[j : j + 1] for j in range(2 * wide // 128)]
            half = len(parts) // 2
            return jnp.concatenate(parts[:half], axis=1), jnp.concatenate(parts[half:], axis=1)

        metas = [meta_of(p) for p in xs]
        right = jnp.concatenate([pad_rows(rows_of(p), wide) for p in xs], axis=0)
        right_cover = jnp.concatenate([m[0] for m in metas], axis=1)
        right_which = jnp.concatenate([m[1] for m in metas], axis=1)
        lane = lax.broadcasted_iota(jnp.int32, (1, wide), 1)
        inside = jnp.concatenate([lane < seg] * len(xs), axis=1)
        right_which = jnp.where(inside, right_which, -1.0)
        cover_cols, which_cols = {}, {}
        first = 0
        for g in range(which_stop):
            for p in range(first, stops[g]):
                part = slice((p - first) * seg, (p - first + 1) * seg)
                cover_cols[p] = old_cols[g][part, :128]
                which_cols[p] = old_cols[g][part, 128:]
            first = stops[g]
        for i, p in enumerate(xs):
            cover_cols[p] = column(metas[i][0])[:seg]
            which_cols[p] = column(metas[i][1])[:seg]
            if not final:
                refs[1][i * seg : (i + 1) * seg, :128] = cover_cols[p]
                refs[1][i * seg : (i + 1) * seg, 128:] = which_cols[p]
        down = jnp.zeros((8, n), jnp.float32)
        total = {}
        for start in range(0, new, per_tile):
            members = range(start, min(start + per_tile, new))
            left = jnp.concatenate([rows_of(p) for p in members], axis=0)
            similar = dot(left, right, NT)
            count = len(members) * seg
            which = jnp.concatenate([which_cols[p] for p in members], axis=0)
            cover = jnp.concatenate([cover_cols[p] for p in members], axis=0)
            similar = jnp.where(repeat(which, n) == right_which, similar, -1e30)
            gain = jnp.maximum(similar - repeat(cover, n), 0.0)
            down = down + jnp.sum(gain.reshape(count // 8, 8, n), axis=0)
            old = [p for p in members if p < done]
            if not old:
                continue
            other = jnp.maximum(similar[: len(old) * seg] - right_cover, 0.0)
            part = other[:, :128]
            for begin in range(128, n, 128):
                part = part + other[:, begin : begin + 128]
            for i, p in enumerate(old):
                mine = pad_rows(part[i * seg : (i + 1) * seg], wide)
                total[p] = jnp.sum(jnp.transpose(mine), axis=0, keepdims=True)
        down = jnp.sum(down, axis=0, keepdims=True)
        for i, p in enumerate(xs):
            total[p] = down[:, i * wide : (i + 1) * wide]
        me = lax.axis_index("clus")
        for p in range(new):
            value = total[p]
            if p < done:
                value = value + gains_ref[p]
            if final:
                out_ref[me ^ offsets[p]] = value
            else:
                out_ref[p] = value

    return kernel


def last_kernel(kernel_devices):
    def kernel(where_ref, gains_ref, out_ref):
        gains = gains_ref[:, 0, :]
        high = gains.astype(jnp.bfloat16)
        rest = gains - high.astype(jnp.float32)
        mid = rest.astype(jnp.bfloat16)
        low = (rest - mid.astype(jnp.float32)).astype(jnp.bfloat16)
        there = hot(where_ref[2:3, :], gains.shape[1])
        found = dot(high, there, NN) + dot(mid, there, NN) + dot(low, there, NN)
        index = lax.broadcasted_iota(jnp.int32, found.shape, 0)
        mine = jnp.where(index == where_ref[1:2, :], found, 0.0)
        out_ref[...] = jnp.sum(mine, axis=0, keepdims=True)

    return kernel


def call(kernel, outs, cost, name, vmem=24, **extra):
    return pl.pallas_call(
        kernel,
        out_shape=outs,
        compiler_params=pltpu.CompilerParams(vmem_limit_bytes=vmem * MIB),
        cost_estimate=pl.CostEstimate(flops=cost[0], bytes_accessed=cost[1], transcendentals=0),
        name=name,
        **extra,
    )


def sequence(devices):
    half = devices // 2
    quarter = max(1, half // 2)
    far = []
    for i in range(quarter):
        far += [half + i, half + quarter + i]
    near = sorted(range(1, half), key=lambda k: (-k.bit_length(), k))
    order = [0, far[0]]
    for i in range(half - 2):
        order += [far[i + 1], near[i]]
    return order + [near[-1], far[-1]]


def body(embeddings, coverage, cluster_ids):
    devices = lax.axis_size("clus")
    rows, width = embeddings.shape
    cap = 2 * rows // (CL_DEV * devices)
    seg = PARTS * cap
    wide = lanes(seg)
    offsets = sequence(devices)
    f32, bf16 = jnp.float32, jnp.bfloat16
    S = jax.ShapeDtypeStruct
    ids = cluster_ids.reshape(1, rows)
    cover = coverage.reshape(rows // 128, 128)
    unitg = devices // 16
    early = EARLY * unitg
    depth = DEPTH * unitg
    tall = width // 128 * seg + TAIL
    piece = S((tall, 128), bf16)

    def pieces_of(count):
        return dict(
            out_specs=[pl.BlockSpec(memory_space=pltpu.HBM)] * count,
            scratch_shapes=[pltpu.VMEM((count, tall, 128), bf16), pltpu.SemaphoreType.DMA((count,))],
        )

    full = pl.BlockSpec(memory_space=pltpu.VMEM)
    hbm = pl.BlockSpec(memory_space=pltpu.HBM)
    steps = 4
    lead = pieces_of(early)
    unit, where, meta, *sent = call(
        first_kernel(devices, cap, steps, offsets[1 : 1 + early]),
        [S((rows, width), bf16), S((3, rows), jnp.int32), S((devices, 1, 2 * wide), f32)] + [piece] * early,
        (2 * early * seg * rows * width, 4 * rows * width),
        "first",
        in_specs=[hbm] * 3,
        out_specs=[hbm] * 3 + lead["out_specs"],
        scratch_shapes=[pltpu.VMEM((1, rows), jnp.int32), pltpu.VMEM((rows // 128, 128), bf16)]
        + [pltpu.VMEM((rows, width), f32), pltpu.VMEM((rows, width), bf16)]
        + [pltpu.VMEM((3, rows), jnp.int32), pltpu.VMEM((devices, 1, 2 * wide), f32)]
        + [lead["scratch_shapes"][0]]
        + [pltpu.SemaphoreType.DMA((steps,))] * 2
        + [lead["scratch_shapes"][1], pltpu.SemaphoreType.DMA((4,))],
        vmem=56,
    )(ids, cover, embeddings)
    for name, ks in (("second", offsets[1 + early : 1 + depth]), ("rest", offsets[1 + depth :] + [0])):
        sent += call(
            rest_kernel(devices, cap, ks),
            [piece] * len(ks),
            (0, 0),
            name,
            in_specs=[full] * 3,
            vmem=20,
            **pieces_of(len(ks)),
        )(where, meta, unit)
    own = sent.pop()

    got = []
    for i, x in enumerate(sent):
        if i >= depth:
            x, got[i - depth] = lax.optimization_barrier((x, got[i - depth]))
        got.append(lax.ppermute(x, "clus", [(d, d ^ offsets[1 + i]) for d in range(devices)]))
    where_from = dict(zip(offsets, [own] + got))
    late = [o for o in offsets if o >= devices // 2][-2:]
    order = [o for o in offsets if o not in late] + late
    pieces = [where_from[o] for o in order]

    gain_shape = S((devices, 1, wide), f32)
    stops = [stop * unitg for stop in STOPS]
    cols, gains = [], []
    for g, new in enumerate(stops):
        fresh = new - (stops[g - 1] if g else 0)
        gains, *more = call(
            gram_kernel(devices, cap, order, stops, g),
            [gain_shape] + [S((fresh * seg, 256), f32)] * (new < devices),
            (2 * new * seg * fresh * seg * width, 2 * new * seg * width),
            "gram",
            vmem=16,
        )(*pieces[:new], *cols, *([gains] if g else []))
        cols += more
    back = lax.all_to_all(gains, "clus", 0, 0, tiled=True)
    out = call(last_kernel(devices), S((1, rows), f32), (2 * rows * wide * 48, 8 * rows), "last")(where, back)
    return out.reshape(rows)


def solution(mesh):
    placed = (P(("parts", "clus"), None), P(("parts", "clus")), P(("parts", "clus"), None))
    return jax.shard_map(
        body, mesh=mesh, in_specs=placed, out_specs=P(("parts", "clus")), check_vma=False
    )
```

```python
import jax
import jax.numpy as jnp
from jax import lax
from jax.experimental import pallas as pl
from jax.experimental.pallas import tpu as pltpu
from jax.sharding import PartitionSpec as P

CL_DEV = 4
PARTS = 3
TAIL = 16
EARLY = 1
DEPTH = 4
STOPS = (4, 6, 8, 10, 12, 14, 15, 16)
MIB = 1024 * 1024

NN = (((1,), (0,)), ((), ()))
NT = (((1,), (1,)), ((), ()))


def dot(left, right, dims):
    return lax.dot_general(left, right, dims, preferred_element_type=jnp.float32)


def lanes(n):
    return -(-n // 128) * 128


def hot(values, count, first=0):
    index = lax.broadcasted_iota(jnp.int32, (count, values.shape[1]), 0) + first
    return jnp.where(index == values, 1.0, 0.0).astype(jnp.bfloat16)


def place(ids, devices, cap):
    rows = ids.shape[1]
    clusters = CL_DEV * devices
    step = 256
    onehot = hot(ids, clusters)
    before = lax.broadcasted_iota(jnp.int32, (step, step), 0) < lax.broadcasted_iota(
        jnp.int32, (step, step), 1
    )
    before = jnp.where(before, 1.0, 0.0).astype(jnp.bfloat16)
    count = jnp.zeros((clusters, 1), jnp.float32)
    ranks = []
    for start in range(0, rows, step):
        piece = onehot[:, start : start + step]
        ranks.append(dot(piece, before, NN) + count)
        count = count + jnp.sum(piece.astype(jnp.float32), axis=1, keepdims=True)
    k = lax.broadcasted_iota(jnp.int32, (clusters, clusters), 0)
    m = lax.broadcasted_iota(jnp.int32, (clusters, clusters), 1)
    j = k % CL_DEV
    plus = (j == 1) & (m == k - 1)
    minus = ((j == 2) & ((m == k) | (m == k + 1))) | ((j == 3) & (m == k))
    mix = (jnp.where(plus, 1.0, 0.0) - jnp.where(minus, 1.0, 0.0)).astype(jnp.bfloat16)
    spread = jnp.broadcast_to(count, (clusters, 128)).astype(jnp.bfloat16)
    base = dot(mix, spread, NN)[:, :1]
    jcol = lax.broadcasted_iota(jnp.int32, (clusters, 1), 0) % CL_DEV
    base = base + jnp.where(jcol >= 2, float(PARTS * cap), 0.0)
    position = []
    for i, start in enumerate(range(0, rows, step)):
        piece = onehot[:, start : start + step].astype(jnp.float32)
        position.append(jnp.sum(piece * (ranks[i] + base), axis=0, keepdims=True))
    return jnp.concatenate(position, axis=1).astype(jnp.int32)


def first_kernel(devices, cap, steps, offsets):
    seg = PARTS * cap
    wide = lanes(seg)

    def kernel(ids_hbm, cover_hbm, emb_ref, unit_ref, where_hbm, meta_hbm, *rest):
        count = len(offsets)
        outs, scratch = rest[:count], rest[count:]
        ids_ref, cover_ref, raw_ref, rows_ref, where_ref, meta_ref, piece_ref = scratch[:7]
        in_sems, rows_sems, out_sems, small_sems = scratch[7:]
        me = lax.axis_index("clus")
        block = raw_ref.shape[0] // steps

        def load(i):
            part = pl.ds(i * block, block)
            return pltpu.make_async_copy(emb_ref.at[part], raw_ref.at[part], in_sems.at[i])

        def store(i):
            part = pl.ds(i * block, block)
            return pltpu.make_async_copy(rows_ref.at[part], unit_ref.at[part], rows_sems.at[i])

        small = [
            pltpu.make_async_copy(ids_hbm, ids_ref, small_sems.at[0]),
            pltpu.make_async_copy(cover_hbm, cover_ref, small_sems.at[1]),
            pltpu.make_async_copy(where_ref, where_hbm, small_sems.at[2]),
            pltpu.make_async_copy(meta_ref, meta_hbm, small_sems.at[3]),
        ]
        small[0].start()
        small[1].start()
        for i in range(steps):
            load(i).start(priority=i % 2)
        small[0].wait()
        small[1].wait()
        ids = ids_ref[...]
        owner = ids // CL_DEV
        position = place(ids, devices, cap)
        code = owner * seg + position
        where_ref[0:1, :] = code
        where_ref[1:2, :] = owner
        where_ref[2:3, :] = position
        own = hot(owner, devices)
        there = hot(position, wide)
        cover = cover_ref[...].astype(jnp.float32)
        cover = jnp.concatenate([cover[i : i + 1] for i in range(cover.shape[0])], axis=1)
        which = (ids - owner * CL_DEV).astype(jnp.float32)
        meta_ref[:, 0, :wide] = dot(own * cover.astype(jnp.bfloat16), there, NT)
        meta_ref[:, 0, wide:] = dot(own * which.astype(jnp.bfloat16), there, NT)
        small[2].start()
        small[3].start()
        for i in range(steps):
            load(i).wait()
            if i == steps - 1:
                for before in range(steps - 1):
                    store(before).start(priority=before % 2)
            raw = raw_ref[i * block : (i + 1) * block, :]
            sums = jnp.sum(raw * raw, axis=-1, keepdims=True)
            unit = (raw * lax.rsqrt(sums + 1e-06)).astype(jnp.bfloat16)
            rows_ref[i * block : (i + 1) * block, :] = unit
        store(steps - 1).start()
        send_pieces(code, rows_ref, meta_ref, seg, me, offsets, outs, piece_ref, out_sems)
        small[2].wait()
        small[3].wait()
        for i in range(steps):
            store(i).wait()

    return kernel


def send_pieces(code, unit_ref, meta_ref, seg, me, offsets, outs, piece_ref, sems):
    copies = []
    slabs = unit_ref.shape[1] // 128
    index = lax.broadcasted_iota(jnp.int32, (TAIL, 128), 0)
    for i, (k, out_ref) in enumerate(zip(offsets, outs)):
        pick = hot(code, seg, (me ^ k) * seg)
        found = dot(pick, unit_ref[...], NN).astype(jnp.bfloat16)
        for f in range(slabs):
            piece_ref[i, f * seg : (f + 1) * seg, :] = found[:, f * 128 : (f + 1) * 128]
        row = meta_ref[me ^ k]
        tail = jnp.zeros((TAIL, 128), jnp.float32)
        for j in range(row.shape[1] // 128):
            tail = jnp.where(index == j, row[:, j * 128 : (j + 1) * 128], tail)
        piece_ref[i, slabs * seg :, :] = tail.astype(jnp.bfloat16)
        copies.append(pltpu.make_async_copy(piece_ref.at[i], out_ref, sems.at[i]))
        copies[-1].start()
    for copy in copies:
        copy.wait()


def rest_kernel(devices, cap, offsets):
    seg = PARTS * cap

    def kernel(where_ref, meta_ref, unit_ref, *rest):
        outs, (piece_ref, sems) = rest[: len(offsets)], rest[len(offsets) :]
        me = lax.axis_index("clus")
        send_pieces(where_ref[0:1, :], unit_ref, meta_ref, seg, me, offsets, outs, piece_ref, sems)

    return kernel


def column(row):
    return jnp.transpose(jnp.broadcast_to(row, (128, row.shape[1])))


def pad_rows(piece, count):
    if piece.shape[0] == count:
        return piece
    fill = jnp.zeros((count - piece.shape[0], piece.shape[1]), piece.dtype)
    return jnp.concatenate([piece, fill], axis=0)


def repeat(col, n):
    return jnp.concatenate([col] * (n // 128), axis=1)


def gram_kernel(devices, cap, offsets, stops, which_stop):
    seg = PARTS * cap
    wide = lanes(seg)
    per_tile = max(1, 768 // seg)
    done = stops[which_stop - 1] if which_stop else 0
    new = stops[which_stop]
    xs = list(range(done, new))
    n = len(xs) * wide
    final = new == devices

    def kernel(*refs):
        pieces, refs = refs[:new], refs[new:]
        old_cols, refs = refs[:which_stop], refs[which_stop:]
        if which_stop:
            gains_ref, refs = refs[0], refs[1:]
        out_ref = refs[0]
        slabs = (pieces[0].shape[0] - TAIL) // seg

        def rows_of(p):
            return jnp.concatenate([pieces[p][f * seg : (f + 1) * seg, :] for f in range(slabs)], axis=1)

        def meta_of(p):
            tail = pieces[p][slabs * seg :, :].astype(jnp.float32)
            parts = [tail[j : j + 1] for j in range(2 * wide // 128)]
            half = len(parts) // 2
            return jnp.concatenate(parts[:half], axis=1), jnp.concatenate(parts[half:], axis=1)

        metas = [meta_of(p) for p in xs]
        right = jnp.concatenate([pad_rows(rows_of(p), wide) for p in xs], axis=0)
        right_cover = jnp.concatenate([m[0] for m in metas], axis=1)
        right_which = jnp.concatenate([m[1] for m in metas], axis=1)
        lane = lax.broadcasted_iota(jnp.int32, (1, wide), 1)
        inside = jnp.concatenate([lane < seg] * len(xs), axis=1)
        right_which = jnp.where(inside, right_which, -1.0)
        cover_cols, which_cols = {}, {}
        first = 0
        for g in range(which_stop):
            for p in range(first, stops[g]):
                part = slice((p - first) * seg, (p - first + 1) * seg)
                cover_cols[p] = old_cols[g][part, :128]
                which_cols[p] = old_cols[g][part, 128:]
            first = stops[g]
        for i, p in enumerate(xs):
            cover_cols[p] = column(metas[i][0])[:seg]
            which_cols[p] = column(metas[i][1])[:seg]
            if not final:
                refs[1][i * seg : (i + 1) * seg, :128] = cover_cols[p]
                refs[1][i * seg : (i + 1) * seg, 128:] = which_cols[p]
        down = jnp.zeros((8, n), jnp.float32)
        total = {}
        for start in range(0, new, per_tile):
            members = range(start, min(start + per_tile, new))
            left = jnp.concatenate([rows_of(p) for p in members], axis=0)
            similar = dot(left, right, NT)
            count = len(members) * seg
            which = jnp.concatenate([which_cols[p] for p in members], axis=0)
            cover = jnp.concatenate([cover_cols[p] for p in members], axis=0)
            similar = jnp.where(repeat(which, n) == right_which, similar, -1e30)
            gain = jnp.maximum(similar - repeat(cover, n), 0.0)
            down = down + jnp.sum(gain.reshape(count // 8, 8, n), axis=0)
            old = [p for p in members if p < done]
            if not old:
                continue
            other = jnp.maximum(similar[: len(old) * seg] - right_cover, 0.0)
            part = other[:, :128]
            for begin in range(128, n, 128):
                part = part + other[:, begin : begin + 128]
            for i, p in enumerate(old):
                mine = pad_rows(part[i * seg : (i + 1) * seg], wide)
                total[p] = jnp.sum(jnp.transpose(mine), axis=0, keepdims=True)
        down = jnp.sum(down, axis=0, keepdims=True)
        for i, p in enumerate(xs):
            total[p] = down[:, i * wide : (i + 1) * wide]
        me = lax.axis_index("clus")
        for p in range(new):
            value = total[p]
            if p < done:
                value = value + gains_ref[p]
            if final:
                out_ref[me ^ offsets[p]] = value
            else:
                out_ref[p] = value

    return kernel


def last_kernel(kernel_devices):
    def kernel(where_ref, gains_ref, out_ref):
        gains = gains_ref[:, 0, :]
        high = gains.astype(jnp.bfloat16)
        rest = gains - high.astype(jnp.float32)
        mid = rest.astype(jnp.bfloat16)
        low = (rest - mid.astype(jnp.float32)).astype(jnp.bfloat16)
        there = hot(where_ref[2:3, :], gains.shape[1])
        found = dot(high, there, NN) + dot(mid, there, NN) + dot(low, there, NN)
        index = lax.broadcasted_iota(jnp.int32, found.shape, 0)
        mine = jnp.where(index == where_ref[1:2, :], found, 0.0)
        out_ref[...] = jnp.sum(mine, axis=0, keepdims=True)

    return kernel


def call(kernel, outs, cost, name, vmem=24, **extra):
    return pl.pallas_call(
        kernel,
        out_shape=outs,
        compiler_params=pltpu.CompilerParams(vmem_limit_bytes=vmem * MIB),
        cost_estimate=pl.CostEstimate(flops=cost[0], bytes_accessed=cost[1], transcendentals=0),
        name=name,
        **extra,
    )


def sequence(devices):
    half = devices // 2
    quarter = max(1, half // 2)
    far = []
    for i in range(quarter):
        far += [half + i, half + quarter + i]
    near = sorted(range(1, half), key=lambda k: (-k.bit_length(), k))
    order = [0, far[0]]
    for i in range(half - 2):
        order += [far[i + 1], near[i]]
    return order + [near[-1], far[-1]]


def body(embeddings, coverage, cluster_ids):
    devices = lax.axis_size("clus")
    rows, width = embeddings.shape
    cap = 2 * rows // (CL_DEV * devices)
    seg = PARTS * cap
    wide = lanes(seg)
    offsets = sequence(devices)
    f32, bf16 = jnp.float32, jnp.bfloat16
    S = jax.ShapeDtypeStruct
    ids = cluster_ids.reshape(1, rows)
    cover = coverage.reshape(rows // 128, 128)
    unitg = devices // 16
    early = EARLY * unitg
    depth = DEPTH * unitg
    tall = width // 128 * seg + TAIL
    piece = S((tall, 128), bf16)

    def pieces_of(count):
        return dict(
            out_specs=[pl.BlockSpec(memory_space=pltpu.HBM)] * count,
            scratch_shapes=[pltpu.VMEM((count, tall, 128), bf16), pltpu.SemaphoreType.DMA((count,))],
        )

    full = pl.BlockSpec(memory_space=pltpu.VMEM)
    hbm = pl.BlockSpec(memory_space=pltpu.HBM)
    steps = 4
    lead = pieces_of(early)
    unit, where, meta, *sent = call(
        first_kernel(devices, cap, steps, offsets[1 : 1 + early]),
        [S((rows, width), bf16), S((3, rows), jnp.int32), S((devices, 1, 2 * wide), f32)] + [piece] * early,
        (2 * early * seg * rows * width, 4 * rows * width),
        "first",
        in_specs=[hbm] * 3,
        out_specs=[hbm] * 3 + lead["out_specs"],
        scratch_shapes=[pltpu.VMEM((1, rows), jnp.int32), pltpu.VMEM((rows // 128, 128), bf16)]
        + [pltpu.VMEM((rows, width), f32), pltpu.VMEM((rows, width), bf16)]
        + [pltpu.VMEM((3, rows), jnp.int32), pltpu.VMEM((devices, 1, 2 * wide), f32)]
        + [lead["scratch_shapes"][0]]
        + [pltpu.SemaphoreType.DMA((steps,))] * 2
        + [lead["scratch_shapes"][1], pltpu.SemaphoreType.DMA((4,))],
        vmem=56,
    )(ids, cover, embeddings)
    for name, ks in (("second", offsets[1 + early : 1 + depth]), ("rest", offsets[1 + depth :] + [0])):
        sent += call(
            rest_kernel(devices, cap, ks),
            [piece] * len(ks),
            (0, 0),
            name,
            in_specs=[full] * 3,
            vmem=20,
            **pieces_of(len(ks)),
        )(where, meta, unit)
    own = sent.pop()

    got = []
    for i, x in enumerate(sent):
        if i >= depth:
            x, got[i - depth] = lax.optimization_barrier((x, got[i - depth]))
        got.append(lax.ppermute(x, "clus", [(d, d ^ offsets[1 + i]) for d in range(devices)]))
    pieces = [own] + got

    gain_shape = S((devices, 1, wide), f32)
    stops = [stop * unitg for stop in STOPS]
    cols, gains = [], []
    for g, new in enumerate(stops):
        fresh = new - (stops[g - 1] if g else 0)
        gains, *more = call(
            gram_kernel(devices, cap, offsets, stops, g),
            [gain_shape] + [S((fresh * seg, 256), f32)] * (new < devices),
            (2 * new * seg * fresh * seg * width, 2 * new * seg * width),
            "gram",
            vmem=16,
        )(*pieces[:new], *cols, *([gains] if g else []))
        cols += more
    back = lax.all_to_all(gains, "clus", 0, 0, tiled=True)
    out = call(last_kernel(devices), S((1, rows), f32), (2 * rows * wide * 48, 8 * rows), "last")(where, back)
    return out.reshape(rows)


def solution(mesh):
    placed = (P(("parts", "clus"), None), P(("parts", "clus")), P(("parts", "clus"), None))
    return jax.shard_map(
        body, mesh=mesh, in_specs=placed, out_specs=P(("parts", "clus")), check_vma=False
    )
```

```python
import jax
import jax.numpy as jnp
from jax import lax
from jax.experimental import pallas as pl
from jax.experimental.pallas import tpu as pltpu
from jax.sharding import PartitionSpec as P

CL_DEV = 4
PARTS = 3
TAIL = 16
EARLY = 1
DEPTH = 4
STOPS = (4, 6, 8, 10, 12, 14, 15, 16)
MIB = 1024 * 1024

NN = (((1,), (0,)), ((), ()))
NT = (((1,), (1,)), ((), ()))


def dot(left, right, dims):
    return lax.dot_general(left, right, dims, preferred_element_type=jnp.float32)


def lanes(n):
    return -(-n // 128) * 128


def hot(values, count, first=0):
    index = lax.broadcasted_iota(jnp.int32, (count, values.shape[1]), 0) + first
    return jnp.where(index == values, 1.0, 0.0).astype(jnp.bfloat16)


def place(ids, devices, cap):
    rows = ids.shape[1]
    clusters = CL_DEV * devices
    step = 256
    onehot = hot(ids, clusters)
    before = lax.broadcasted_iota(jnp.int32, (step, step), 0) < lax.broadcasted_iota(
        jnp.int32, (step, step), 1
    )
    before = jnp.where(before, 1.0, 0.0).astype(jnp.bfloat16)
    count = jnp.zeros((clusters, 1), jnp.float32)
    ranks = []
    for start in range(0, rows, step):
        piece = onehot[:, start : start + step]
        ranks.append(dot(piece, before, NN) + count)
        count = count + jnp.sum(piece.astype(jnp.float32), axis=1, keepdims=True)
    k = lax.broadcasted_iota(jnp.int32, (clusters, clusters), 0)
    m = lax.broadcasted_iota(jnp.int32, (clusters, clusters), 1)
    j = k % CL_DEV
    plus = (j == 1) & (m == k - 1)
    minus = ((j == 2) & ((m == k) | (m == k + 1))) | ((j == 3) & (m == k))
    mix = (jnp.where(plus, 1.0, 0.0) - jnp.where(minus, 1.0, 0.0)).astype(jnp.bfloat16)
    spread = jnp.broadcast_to(count, (clusters, 128)).astype(jnp.bfloat16)
    base = dot(mix, spread, NN)[:, :1]
    jcol = lax.broadcasted_iota(jnp.int32, (clusters, 1), 0) % CL_DEV
    base = base + jnp.where(jcol >= 2, float(PARTS * cap), 0.0)
    position = []
    for i, start in enumerate(range(0, rows, step)):
        piece = onehot[:, start : start + step].astype(jnp.float32)
        position.append(jnp.sum(piece * (ranks[i] + base), axis=0, keepdims=True))
    return jnp.concatenate(position, axis=1).astype(jnp.int32)


def first_kernel(devices, cap, steps, offsets):
    seg = PARTS * cap
    wide = lanes(seg)

    def kernel(ids_hbm, cover_hbm, emb_ref, unit_ref, where_hbm, meta_hbm, *rest):
        count = len(offsets)
        outs, scratch = rest[:count], rest[count:]
        ids_ref, cover_ref, raw_ref, rows_ref, where_ref, meta_ref, piece_ref = scratch[:7]
        in_sems, rows_sems, out_sems, small_sems = scratch[7:]
        me = lax.axis_index("clus")
        block = raw_ref.shape[0] // steps

        def load(i):
            part = pl.ds(i * block, block)
            return pltpu.make_async_copy(emb_ref.at[part], raw_ref.at[part], in_sems.at[i])

        def store(i):
            part = pl.ds(i * block, block)
            return pltpu.make_async_copy(rows_ref.at[part], unit_ref.at[part], rows_sems.at[i])

        small = [
            pltpu.make_async_copy(ids_hbm, ids_ref, small_sems.at[0]),
            pltpu.make_async_copy(cover_hbm, cover_ref, small_sems.at[1]),
            pltpu.make_async_copy(where_ref, where_hbm, small_sems.at[2]),
            pltpu.make_async_copy(meta_ref, meta_hbm, small_sems.at[3]),
        ]
        small[0].start()
        small[1].start()
        for i in range(steps):
            load(i).start(priority=i % 2)
        small[0].wait()
        small[1].wait()
        ids = ids_ref[...]
        owner = ids // CL_DEV
        position = place(ids, devices, cap)
        code = owner * seg + position
        where_ref[0:1, :] = code
        where_ref[1:2, :] = owner
        where_ref[2:3, :] = position
        own = hot(owner, devices)
        there = hot(position, wide)
        cover = cover_ref[...].astype(jnp.float32)
        cover = jnp.concatenate([cover[i : i + 1] for i in range(cover.shape[0])], axis=1)
        which = (ids - owner * CL_DEV).astype(jnp.float32)
        meta_ref[:, 0, :wide] = dot(own * cover.astype(jnp.bfloat16), there, NT)
        meta_ref[:, 0, wide:] = dot(own * which.astype(jnp.bfloat16), there, NT)
        small[2].start()
        small[3].start()
        for i in range(steps):
            load(i).wait()
            if i == steps - 1:
                for before in range(steps - 1):
                    store(before).start(priority=before % 2)
            raw = raw_ref[i * block : (i + 1) * block, :]
            sums = jnp.sum(raw * raw, axis=-1, keepdims=True)
            unit = (raw * lax.rsqrt(sums + 1e-06)).astype(jnp.bfloat16)
            rows_ref[i * block : (i + 1) * block, :] = unit
        store(steps - 1).start()
        send_pieces(code, rows_ref, meta_ref, seg, me, offsets, outs, piece_ref, out_sems)
        small[2].wait()
        small[3].wait()
        for i in range(steps):
            store(i).wait()

    return kernel


def send_pieces(code, unit_ref, meta_ref, seg, me, offsets, outs, piece_ref, sems):
    copies = []
    slabs = unit_ref.shape[1] // 128
    index = lax.broadcasted_iota(jnp.int32, (TAIL, 128), 0)
    for i, (k, out_ref) in enumerate(zip(offsets, outs)):
        pick = hot(code, seg, (me ^ k) * seg)
        found = dot(pick, unit_ref[...], NN).astype(jnp.bfloat16)
        for f in range(slabs):
            piece_ref[i, f * seg : (f + 1) * seg, :] = found[:, f * 128 : (f + 1) * 128]
        row = meta_ref[me ^ k]
        tail = jnp.zeros((TAIL, 128), jnp.float32)
        for j in range(row.shape[1] // 128):
            tail = jnp.where(index == j, row[:, j * 128 : (j + 1) * 128], tail)
        piece_ref[i, slabs * seg :, :] = tail.astype(jnp.bfloat16)
        copies.append(pltpu.make_async_copy(piece_ref.at[i], out_ref, sems.at[i]))
        copies[-1].start()
    for copy in copies:
        copy.wait()


def rest_kernel(devices, cap, offsets):
    seg = PARTS * cap

    def kernel(where_ref, meta_ref, unit_ref, *rest):
        outs, (piece_ref, sems) = rest[: len(offsets)], rest[len(offsets) :]
        me = lax.axis_index("clus")
        send_pieces(where_ref[0:1, :], unit_ref, meta_ref, seg, me, offsets, outs, piece_ref, sems)

    return kernel


def column(row):
    return jnp.transpose(jnp.broadcast_to(row, (128, row.shape[1])))


def pad_rows(piece, count):
    if piece.shape[0] == count:
        return piece
    fill = jnp.zeros((count - piece.shape[0], piece.shape[1]), piece.dtype)
    return jnp.concatenate([piece, fill], axis=0)


def repeat(col, n):
    return jnp.concatenate([col] * (n // 128), axis=1)


def gram_kernel(devices, cap, offsets, stops, which_stop):
    seg = PARTS * cap
    wide = lanes(seg)
    per_tile = max(1, 768 // seg)
    done = stops[which_stop - 1] if which_stop else 0
    new = stops[which_stop]
    xs = list(range(done, new))
    n = len(xs) * wide
    final = new == devices

    def kernel(*refs):
        pieces, refs = refs[:new], refs[new:]
        old_cols, refs = refs[:which_stop], refs[which_stop:]
        if which_stop:
            gains_ref, refs = refs[0], refs[1:]
        out_ref = refs[0]
        slabs = (pieces[0].shape[0] - TAIL) // seg

        def rows_of(p):
            return jnp.concatenate([pieces[p][f * seg : (f + 1) * seg, :] for f in range(slabs)], axis=1)

        def meta_of(p):
            tail = pieces[p][slabs * seg :, :].astype(jnp.float32)
            parts = [tail[j : j + 1] for j in range(2 * wide // 128)]
            half = len(parts) // 2
            return jnp.concatenate(parts[:half], axis=1), jnp.concatenate(parts[half:], axis=1)

        metas = [meta_of(p) for p in xs]
        right = jnp.concatenate([pad_rows(rows_of(p), wide) for p in xs], axis=0)
        right_cover = jnp.concatenate([m[0] for m in metas], axis=1)
        right_which = jnp.concatenate([m[1] for m in metas], axis=1)
        lane = lax.broadcasted_iota(jnp.int32, (1, wide), 1)
        inside = jnp.concatenate([lane < seg] * len(xs), axis=1)
        right_which = jnp.where(inside, right_which, -1.0)
        cover_cols, which_cols = {}, {}
        first = 0
        for g in range(which_stop):
            for p in range(first, stops[g]):
                part = slice((p - first) * seg, (p - first + 1) * seg)
                cover_cols[p] = old_cols[g][part, :128]
                which_cols[p] = old_cols[g][part, 128:]
            first = stops[g]
        for i, p in enumerate(xs):
            cover_cols[p] = column(metas[i][0])[:seg]
            which_cols[p] = column(metas[i][1])[:seg]
            if not final:
                refs[1][i * seg : (i + 1) * seg, :128] = cover_cols[p]
                refs[1][i * seg : (i + 1) * seg, 128:] = which_cols[p]
        down = jnp.zeros((8, n), jnp.float32)
        total = {}
        for start in range(0, new, per_tile):
            members = range(start, min(start + per_tile, new))
            left = jnp.concatenate([rows_of(p) for p in members], axis=0)
            similar = dot(left, right, NT)
            count = len(members) * seg
            which = jnp.concatenate([which_cols[p] for p in members], axis=0)
            cover = jnp.concatenate([cover_cols[p] for p in members], axis=0)
            similar = jnp.where(repeat(which, n) == right_which, similar, -1e30)
            gain = jnp.maximum(similar - repeat(cover, n), 0.0)
            down = down + jnp.sum(gain.reshape(count // 8, 8, n), axis=0)
            old = [p for p in members if p < done]
            if not old:
                continue
            other = jnp.maximum(similar[: len(old) * seg] - right_cover, 0.0)
            part = other[:, :128]
            for begin in range(128, n, 128):
                part = part + other[:, begin : begin + 128]
            for i, p in enumerate(old):
                mine = pad_rows(part[i * seg : (i + 1) * seg], wide)
                total[p] = jnp.sum(jnp.transpose(mine), axis=0, keepdims=True)
        down = jnp.sum(down, axis=0, keepdims=True)
        for i, p in enumerate(xs):
            total[p] = down[:, i * wide : (i + 1) * wide]
        me = lax.axis_index("clus")
        for p in range(new):
            value = total[p]
            if p < done:
                value = value + gains_ref[p]
            if final:
                out_ref[me ^ offsets[p]] = value
            else:
                out_ref[p] = value

    return kernel


def last_kernel(kernel_devices):
    def kernel(where_ref, gains_ref, out_ref):
        gains = gains_ref[:, 0, :]
        high = gains.astype(jnp.bfloat16)
        rest = gains - high.astype(jnp.float32)
        mid = rest.astype(jnp.bfloat16)
        low = (rest - mid.astype(jnp.float32)).astype(jnp.bfloat16)
        there = hot(where_ref[2:3, :], gains.shape[1])
        found = dot(high, there, NN) + dot(mid, there, NN) + dot(low, there, NN)
        index = lax.broadcasted_iota(jnp.int32, found.shape, 0)
        mine = jnp.where(index == where_ref[1:2, :], found, 0.0)
        out_ref[...] = jnp.sum(mine, axis=0, keepdims=True)

    return kernel


def call(kernel, outs, cost, name, vmem=24, **extra):
    return pl.pallas_call(
        kernel,
        out_shape=outs,
        compiler_params=pltpu.CompilerParams(vmem_limit_bytes=vmem * MIB),
        cost_estimate=pl.CostEstimate(flops=cost[0], bytes_accessed=cost[1], transcendentals=0),
        name=name,
        **extra,
    )


def sequence(devices):
    half = devices // 2
    quarter = half // 2
    far = []
    for i in range(quarter):
        far += [half + i, half + quarter + i]
    near = sorted(range(4, half), key=lambda k: (-k.bit_length(), k))
    chain = [far[0]]
    for i, k in enumerate(near):
        chain += [far[i + 1], k]
    return chain + far[len(near) + 1 :]


def body(embeddings, coverage, cluster_ids):
    devices = lax.axis_size("clus")
    rows, width = embeddings.shape
    cap = 2 * rows // (CL_DEV * devices)
    seg = PARTS * cap
    wide = lanes(seg)
    chain = sequence(devices)
    f32, bf16 = jnp.float32, jnp.bfloat16
    S = jax.ShapeDtypeStruct
    ids = cluster_ids.reshape(1, rows)
    cover = coverage.reshape(rows // 128, 128)
    unitg = devices // 16
    early = EARLY * unitg
    depth = DEPTH * unitg
    tall = width // 128 * seg + TAIL
    piece = S((tall, 128), bf16)

    def pieces_of(count):
        return dict(
            out_specs=[pl.BlockSpec(memory_space=pltpu.HBM)] * count,
            scratch_shapes=[pltpu.VMEM((count, tall, 128), bf16), pltpu.SemaphoreType.DMA((count,))],
        )

    full = pl.BlockSpec(memory_space=pltpu.VMEM)
    hbm = pl.BlockSpec(memory_space=pltpu.HBM)
    steps = 4
    lead = pieces_of(early)
    unit, where, meta, *sent = call(
        first_kernel(devices, cap, steps, chain[:early]),
        [S((rows, width), bf16), S((3, rows), jnp.int32), S((devices, 1, 2 * wide), f32)] + [piece] * early,
        (2 * early * seg * rows * width, 4 * rows * width),
        "first",
        in_specs=[hbm] * 3,
        out_specs=[hbm] * 3 + lead["out_specs"],
        scratch_shapes=[pltpu.VMEM((1, rows), jnp.int32), pltpu.VMEM((rows // 128, 128), bf16)]
        + [pltpu.VMEM((rows, width), f32), pltpu.VMEM((rows, width), bf16)]
        + [pltpu.VMEM((3, rows), jnp.int32), pltpu.VMEM((devices, 1, 2 * wide), f32)]
        + [lead["scratch_shapes"][0]]
        + [pltpu.SemaphoreType.DMA((steps,))] * 2
        + [lead["scratch_shapes"][1], pltpu.SemaphoreType.DMA((4,))],
        vmem=56,
    )(ids, cover, embeddings)
    for name, ks in (("second", chain[early:depth]), ("rest", chain[depth:] + [2, 3, 1, 0])):
        sent += call(
            rest_kernel(devices, cap, ks),
            [piece] * len(ks),
            (len(ks) * 2 * seg * rows * width, 0),
            name,
            in_specs=[full] * 3,
            vmem=20,
            **pieces_of(len(ks)),
        )(where, meta, unit)
    pieces = dict(zip(chain + [2, 3, 1, 0], sent))
    leader = {k: chain[i] for i, k in enumerate(chain[depth:])}
    leader.update({2: chain[3 * unitg], 3: chain[5 * unitg], 1: chain[7 * unitg]})
    for k in chain + [2, 3, 1]:
        x = pieces[k]
        if k in leader:
            x, pieces[leader[k]] = lax.optimization_barrier((x, pieces[leader[k]]))
        pieces[k] = lax.ppermute(x, "clus", [(d, d ^ k) for d in range(devices)])
    order = [0] + chain[:-5] + [2, 3] + chain[-5:-3] + [1] + chain[-3:]
    pieces = [pieces[k] for k in order]

    gain_shape = S((devices, 1, wide), f32)
    stops = [stop * unitg for stop in STOPS]
    cols, gains = [], []
    for g, new in enumerate(stops):
        fresh = new - (stops[g - 1] if g else 0)
        gains, *more = call(
            gram_kernel(devices, cap, order, stops, g),
            [gain_shape] + [S((fresh * seg, 256), f32)] * (new < devices),
            (2 * new * seg * fresh * seg * width, 2 * new * seg * width),
            "gram",
            vmem=16,
        )(*pieces[:new], *cols, *([gains] if g else []))
        cols += more
    back = lax.all_to_all(gains, "clus", 0, 0, tiled=True)
    out = call(last_kernel(devices), S((1, rows), f32), (2 * rows * wide * 48, 8 * rows), "last")(where, back)
    return out.reshape(rows)


def solution(mesh):
    placed = (P(("parts", "clus"), None), P(("parts", "clus")), P(("parts", "clus"), None))
    return jax.shard_map(
        body, mesh=mesh, in_specs=placed, out_specs=P(("parts", "clus")), check_vma=False
    )
```

```python
import jax
import jax.numpy as jnp
from jax import lax
from jax.experimental import pallas as pl
from jax.experimental.pallas import tpu as pltpu
from jax.sharding import PartitionSpec as P

CL_DEV = 4
PARTS = 3
TAIL = 16
EARLY = 1
DEPTH = 4
STOPS = (4, 6, 8, 10, 12, 14, 15, 16)
MIB = 1024 * 1024

NN = (((1,), (0,)), ((), ()))
NT = (((1,), (1,)), ((), ()))


def dot(left, right, dims):
    return lax.dot_general(left, right, dims, preferred_element_type=jnp.float32)


def lanes(n):
    return -(-n // 128) * 128


def hot(values, count, first=0):
    index = lax.broadcasted_iota(jnp.int32, (count, values.shape[1]), 0) + first
    return jnp.where(index == values, 1.0, 0.0).astype(jnp.bfloat16)


def place(ids, devices, cap):
    rows = ids.shape[1]
    clusters = CL_DEV * devices
    step = 256
    onehot = hot(ids, clusters)
    before = lax.broadcasted_iota(jnp.int32, (step, step), 0) < lax.broadcasted_iota(
        jnp.int32, (step, step), 1
    )
    before = jnp.where(before, 1.0, 0.0).astype(jnp.bfloat16)
    count = jnp.zeros((clusters, 1), jnp.float32)
    ranks = []
    for start in range(0, rows, step):
        piece = onehot[:, start : start + step]
        ranks.append(dot(piece, before, NN) + count)
        count = count + jnp.sum(piece.astype(jnp.float32), axis=1, keepdims=True)
    k = lax.broadcasted_iota(jnp.int32, (clusters, clusters), 0)
    m = lax.broadcasted_iota(jnp.int32, (clusters, clusters), 1)
    j = k % CL_DEV
    plus = (j == 1) & (m == k - 1)
    minus = ((j == 2) & ((m == k) | (m == k + 1))) | ((j == 3) & (m == k))
    mix = (jnp.where(plus, 1.0, 0.0) - jnp.where(minus, 1.0, 0.0)).astype(jnp.bfloat16)
    spread = jnp.broadcast_to(count, (clusters, 128)).astype(jnp.bfloat16)
    base = dot(mix, spread, NN)[:, :1]
    jcol = lax.broadcasted_iota(jnp.int32, (clusters, 1), 0) % CL_DEV
    base = base + jnp.where(jcol >= 2, float(PARTS * cap), 0.0)
    position = []
    for i, start in enumerate(range(0, rows, step)):
        piece = onehot[:, start : start + step].astype(jnp.float32)
        position.append(jnp.sum(piece * (ranks[i] + base), axis=0, keepdims=True))
    return jnp.concatenate(position, axis=1).astype(jnp.int32)


def first_kernel(devices, cap, steps, offsets):
    seg = PARTS * cap
    wide = lanes(seg)

    def kernel(ids_hbm, cover_hbm, emb_ref, unit_ref, where_hbm, meta_hbm, *rest):
        count = len(offsets)
        outs, scratch = rest[:count], rest[count:]
        ids_ref, cover_ref, raw_ref, rows_ref, where_ref, meta_ref, piece_ref = scratch[:7]
        in_sems, rows_sems, out_sems, small_sems = scratch[7:]
        me = lax.axis_index("clus")
        block = raw_ref.shape[0] // steps

        def load(i):
            part = pl.ds(i * block, block)
            return pltpu.make_async_copy(emb_ref.at[part], raw_ref.at[part], in_sems.at[i])

        def store(i):
            part = pl.ds(i * block, block)
            return pltpu.make_async_copy(rows_ref.at[part], unit_ref.at[part], rows_sems.at[i])

        small = [
            pltpu.make_async_copy(ids_hbm, ids_ref, small_sems.at[0]),
            pltpu.make_async_copy(cover_hbm, cover_ref, small_sems.at[1]),
            pltpu.make_async_copy(where_ref, where_hbm, small_sems.at[2]),
            pltpu.make_async_copy(meta_ref, meta_hbm, small_sems.at[3]),
        ]
        small[0].start()
        small[1].start()
        for i in range(steps):
            load(i).start(priority=i % 2)
        small[0].wait()
        small[1].wait()
        ids = ids_ref[...]
        owner = ids // CL_DEV
        position = place(ids, devices, cap)
        code = owner * seg + position
        where_ref[0:1, :] = code
        where_ref[1:2, :] = owner
        where_ref[2:3, :] = position
        own = hot(owner, devices)
        there = hot(position, wide)
        cover = cover_ref[...].astype(jnp.float32)
        cover = jnp.concatenate([cover[i : i + 1] for i in range(cover.shape[0])], axis=1)
        which = (ids - owner * CL_DEV).astype(jnp.float32)
        meta_ref[:, 0, :wide] = dot(own * cover.astype(jnp.bfloat16), there, NT)
        meta_ref[:, 0, wide:] = dot(own * which.astype(jnp.bfloat16), there, NT)
        small[2].start()
        small[3].start()
        for i in range(steps):
            load(i).wait()
            if i == steps - 1:
                for before in range(steps - 1):
                    store(before).start(priority=before % 2)
            raw = raw_ref[i * block : (i + 1) * block, :]
            sums = jnp.sum(raw * raw, axis=-1, keepdims=True)
            unit = (raw * lax.rsqrt(sums + 1e-06)).astype(jnp.bfloat16)
            rows_ref[i * block : (i + 1) * block, :] = unit
        store(steps - 1).start()
        send_pieces(code, rows_ref, meta_ref, seg, me, offsets, outs, piece_ref, out_sems)
        small[2].wait()
        small[3].wait()
        for i in range(steps):
            store(i).wait()

    return kernel


def send_pieces(code, unit_ref, meta_ref, seg, me, offsets, outs, piece_ref, sems):
    copies = []
    slabs = unit_ref.shape[1] // 128
    index = lax.broadcasted_iota(jnp.int32, (TAIL, 128), 0)
    for i, (k, out_ref) in enumerate(zip(offsets, outs)):
        pick = hot(code, seg, (me ^ k) * seg)
        found = dot(pick, unit_ref[...], NN).astype(jnp.bfloat16)
        for f in range(slabs):
            piece_ref[i, f * seg : (f + 1) * seg, :] = found[:, f * 128 : (f + 1) * 128]
        row = meta_ref[me ^ k]
        tail = jnp.zeros((TAIL, 128), jnp.float32)
        for j in range(row.shape[1] // 128):
            tail = jnp.where(index == j, row[:, j * 128 : (j + 1) * 128], tail)
        piece_ref[i, slabs * seg :, :] = tail.astype(jnp.bfloat16)
        copies.append(pltpu.make_async_copy(piece_ref.at[i], out_ref, sems.at[i]))
        copies[-1].start()
    for copy in copies:
        copy.wait()


def rest_kernel(devices, cap, offsets):
    seg = PARTS * cap

    def kernel(where_ref, meta_ref, unit_ref, *rest):
        outs, (piece_ref, sems) = rest[: len(offsets)], rest[len(offsets) :]
        me = lax.axis_index("clus")
        send_pieces(where_ref[0:1, :], unit_ref, meta_ref, seg, me, offsets, outs, piece_ref, sems)

    return kernel


def column(row):
    return jnp.transpose(jnp.broadcast_to(row, (128, row.shape[1])))


def pad_rows(piece, count):
    if piece.shape[0] == count:
        return piece
    fill = jnp.zeros((count - piece.shape[0], piece.shape[1]), piece.dtype)
    return jnp.concatenate([piece, fill], axis=0)


def repeat(col, n):
    return jnp.concatenate([col] * (n // 128), axis=1)


def gram_kernel(devices, cap, offsets, stops, which_stop):
    seg = PARTS * cap
    wide = lanes(seg)
    per_tile = max(1, 768 // cap)
    done = stops[which_stop - 1] if which_stop else 0
    new = stops[which_stop]
    xs = list(range(done, new))
    m = len(xs)
    meets = ((0, 1), (0, 1, 2), (1, 2))
    final = new == devices

    def kernel(*refs):
        pieces, refs = refs[:new], refs[new:]
        old_cols, refs = refs[:which_stop], refs[which_stop:]
        if which_stop:
            gains_ref, refs = refs[0], refs[1:]
        out_ref = refs[0]
        slabs = (pieces[0].shape[0] - TAIL) // seg

        def chunk(p, c):
            rows = [pieces[p][f * seg + c * cap : f * seg + (c + 1) * cap, :] for f in range(slabs)]
            return jnp.concatenate(rows, axis=1)

        def meta_of(p):
            tail = pieces[p][slabs * seg :, :].astype(jnp.float32)
            parts = [tail[j : j + 1] for j in range(2 * wide // 128)]
            half = len(parts) // 2
            return jnp.concatenate(parts[:half], axis=1), jnp.concatenate(parts[half:], axis=1)

        metas = [meta_of(p) for p in xs]
        right, right_cover, right_which, down = [], [], [], []
        for meet in meets:
            n = lanes(len(meet) * m * cap)
            fill = [jnp.full((1, n - len(meet) * m * cap), -1.0, jnp.float32)]
            fill = fill if fill[0].shape[1] else []
            right.append(pad_rows(jnp.concatenate([chunk(p, c) for c in meet for p in xs], axis=0), n))
            rows = [[meta[v][:, c * cap : (c + 1) * cap] for c in meet for meta in metas] for v in (0, 1)]
            right_cover.append(jnp.concatenate(rows[0] + fill, axis=1))
            right_which.append(jnp.concatenate(rows[1] + fill, axis=1))
            down.append(jnp.zeros((8, n), jnp.float32))
        cover_cols, which_cols = {}, {}
        first = 0
        for g in range(which_stop):
            for p in range(first, stops[g]):
                part = slice((p - first) * seg, (p - first + 1) * seg)
                cover_cols[p] = old_cols[g][part, :128]
                which_cols[p] = old_cols[g][part, 128:]
            first = stops[g]
        for i, p in enumerate(xs):
            cover_cols[p] = column(metas[i][0])[:seg]
            which_cols[p] = column(metas[i][1])[:seg]
            if not final:
                refs[1][i * seg : (i + 1) * seg, :128] = cover_cols[p]
                refs[1][i * seg : (i + 1) * seg, 128:] = which_cols[p]
        total, found = {}, {}
        for start in range(0, new, per_tile):
            members = range(start, min(start + per_tile, new))
            old = [p for p in members if p < done]
            for c, meet in enumerate(meets):
                n = right[c].shape[0]
                part = slice(c * cap, (c + 1) * cap)
                left = jnp.concatenate([chunk(p, c) for p in members], axis=0)
                similar = dot(left, right[c], NT)
                which = jnp.concatenate([which_cols[p][part] for p in members], axis=0)
                cover = jnp.concatenate([cover_cols[p][part] for p in members], axis=0)
                similar = jnp.where(repeat(which, n) == right_which[c], similar, -1e30)
                gain = jnp.maximum(similar - repeat(cover, n), 0.0)
                down[c] = down[c] + jnp.sum(gain.reshape(left.shape[0] // 8, 8, n), axis=0)
                if not old:
                    continue
                other = jnp.maximum(similar[: len(old) * cap] - right_cover[c], 0.0)
                folded = other[:, :128]
                for begin in range(128, n, 128):
                    folded = folded + other[:, begin : begin + 128]
                for i, p in enumerate(old):
                    found[p, c] = folded[i * cap : (i + 1) * cap]
        for p in range(done):
            mine = pad_rows(jnp.concatenate([found[p, c] for c in range(PARTS)], axis=0), wide)
            total[p] = jnp.sum(jnp.transpose(mine), axis=0, keepdims=True)
        down = [jnp.sum(d, axis=0, keepdims=True) for d in down]
        for i, p in enumerate(xs):
            values = []
            for c in range(PARTS):
                value = jnp.zeros((1, cap), jnp.float32)
                for d, meet in zip(down, meets):
                    if c in meet:
                        begin = (meet.index(c) * m + i) * cap
                        value = value + d[:, begin : begin + cap]
                values.append(value)
            if wide > seg:
                values.append(jnp.zeros((1, wide - seg), jnp.float32))
            total[p] = jnp.concatenate(values, axis=1)
        me = lax.axis_index("clus")
        for p in range(new):
            value = total[p]
            if p < done:
                value = value + gains_ref[p]
            if final:
                out_ref[me ^ offsets[p]] = value
            else:
                out_ref[p] = value

    return kernel


def last_kernel(kernel_devices):
    def kernel(where_ref, gains_ref, out_ref):
        gains = gains_ref[:, 0, :]
        high = gains.astype(jnp.bfloat16)
        rest = gains - high.astype(jnp.float32)
        mid = rest.astype(jnp.bfloat16)
        low = (rest - mid.astype(jnp.float32)).astype(jnp.bfloat16)
        there = hot(where_ref[2:3, :], gains.shape[1])
        found = dot(high, there, NN) + dot(mid, there, NN) + dot(low, there, NN)
        index = lax.broadcasted_iota(jnp.int32, found.shape, 0)
        mine = jnp.where(index == where_ref[1:2, :], found, 0.0)
        out_ref[...] = jnp.sum(mine, axis=0, keepdims=True)

    return kernel


def call(kernel, outs, cost, name, vmem=24, **extra):
    return pl.pallas_call(
        kernel,
        out_shape=outs,
        compiler_params=pltpu.CompilerParams(vmem_limit_bytes=vmem * MIB),
        cost_estimate=pl.CostEstimate(flops=cost[0], bytes_accessed=cost[1], transcendentals=0),
        name=name,
        **extra,
    )


def sequence(devices):
    half = devices // 2
    quarter = max(1, half // 2)
    far = []
    for i in range(quarter):
        far += [half + i, half + quarter + i]
    near = sorted(range(1, half), key=lambda k: (-k.bit_length(), k))
    order = [0, far[0]]
    for i in range(half - 2):
        order += [far[i + 1], near[i]]
    return order + [near[-1], far[-1]]


def body(embeddings, coverage, cluster_ids):
    devices = lax.axis_size("clus")
    rows, width = embeddings.shape
    cap = 2 * rows // (CL_DEV * devices)
    seg = PARTS * cap
    wide = lanes(seg)
    offsets = sequence(devices)
    f32, bf16 = jnp.float32, jnp.bfloat16
    S = jax.ShapeDtypeStruct
    ids = cluster_ids.reshape(1, rows)
    cover = coverage.reshape(rows // 128, 128)
    unitg = devices // 16
    early = EARLY * unitg
    depth = DEPTH * unitg
    tall = width // 128 * seg + TAIL
    piece = S((tall, 128), bf16)

    def pieces_of(count):
        return dict(
            out_specs=[pl.BlockSpec(memory_space=pltpu.HBM)] * count,
            scratch_shapes=[pltpu.VMEM((count, tall, 128), bf16), pltpu.SemaphoreType.DMA((count,))],
        )

    full = pl.BlockSpec(memory_space=pltpu.VMEM)
    hbm = pl.BlockSpec(memory_space=pltpu.HBM)
    steps = 4
    lead = pieces_of(early)
    unit, where, meta, *sent = call(
        first_kernel(devices, cap, steps, offsets[1 : 1 + early]),
        [S((rows, width), bf16), S((3, rows), jnp.int32), S((devices, 1, 2 * wide), f32)] + [piece] * early,
        (2 * early * seg * rows * width, 4 * rows * width),
        "first",
        in_specs=[hbm] * 3,
        out_specs=[hbm] * 3 + lead["out_specs"],
        scratch_shapes=[pltpu.VMEM((1, rows), jnp.int32), pltpu.VMEM((rows // 128, 128), bf16)]
        + [pltpu.VMEM((rows, width), f32), pltpu.VMEM((rows, width), bf16)]
        + [pltpu.VMEM((3, rows), jnp.int32), pltpu.VMEM((devices, 1, 2 * wide), f32)]
        + [lead["scratch_shapes"][0]]
        + [pltpu.SemaphoreType.DMA((steps,))] * 2
        + [lead["scratch_shapes"][1], pltpu.SemaphoreType.DMA((4,))],
        vmem=56,
    )(ids, cover, embeddings)
    for name, ks in (("second", offsets[1 + early : 1 + depth]), ("rest", offsets[1 + depth :] + [0])):
        sent += call(
            rest_kernel(devices, cap, ks),
            [piece] * len(ks),
            (0, 0),
            name,
            in_specs=[full] * 3,
            vmem=20,
            **pieces_of(len(ks)),
        )(where, meta, unit)
    own = sent.pop()

    got = []
    for i, x in enumerate(sent):
        if i >= depth:
            x, got[i - depth] = lax.optimization_barrier((x, got[i - depth]))
        got.append(lax.ppermute(x, "clus", [(d, d ^ offsets[1 + i]) for d in range(devices)]))
    pieces = [own] + got

    gain_shape = S((devices, 1, wide), f32)
    stops = [stop * unitg for stop in STOPS]
    cols, gains = [], []
    for g, new in enumerate(stops):
        fresh = new - (stops[g - 1] if g else 0)
        gains, *more = call(
            gram_kernel(devices, cap, offsets, stops, g),
            [gain_shape] + [S((fresh * seg, 256), f32)] * (new < devices),
            (2 * new * seg * fresh * seg * width, 2 * new * seg * width),
            "gram",
            vmem=16,
        )(*pieces[:new], *cols, *([gains] if g else []))
        cols += more
    back = lax.all_to_all(gains, "clus", 0, 0, tiled=True)
    out = call(last_kernel(devices), S((1, rows), f32), (2 * rows * wide * 48, 8 * rows), "last")(where, back)
    return out.reshape(rows)


def solution(mesh):
    placed = (P(("parts", "clus"), None), P(("parts", "clus")), P(("parts", "clus"), None))
    return jax.shard_map(
        body, mesh=mesh, in_specs=placed, out_specs=P(("parts", "clus")), check_vma=False
    )
```

```python
import jax
import jax.numpy as jnp
from jax import lax
from jax.experimental import pallas as pl
from jax.experimental.pallas import tpu as pltpu
from jax.sharding import PartitionSpec as P

CL_DEV = 4
PARTS = 3
TAIL = 16
EARLY = 1
DEPTH = 4
STOPS = (4, 6, 8, 10, 12, 14, 15, 16)
MIB = 1024 * 1024

NN = (((1,), (0,)), ((), ()))
NT = (((1,), (1,)), ((), ()))


def dot(left, right, dims):
    return lax.dot_general(left, right, dims, preferred_element_type=jnp.float32)


def lanes(n):
    return -(-n // 128) * 128


def hot(values, count, first=0):
    index = lax.broadcasted_iota(jnp.int32, (count, values.shape[1]), 0) + first
    return jnp.where(index == values, 1.0, 0.0).astype(jnp.bfloat16)


def place(ids, devices, cap):
    rows = ids.shape[1]
    clusters = CL_DEV * devices
    step = 256
    onehot = hot(ids, clusters)
    before = lax.broadcasted_iota(jnp.int32, (step, step), 0) < lax.broadcasted_iota(
        jnp.int32, (step, step), 1
    )
    before = jnp.where(before, 1.0, 0.0).astype(jnp.bfloat16)
    count = jnp.zeros((clusters, 1), jnp.float32)
    ranks = []
    for start in range(0, rows, step):
        piece = onehot[:, start : start + step]
        ranks.append(dot(piece, before, NN) + count)
        count = count + jnp.sum(piece.astype(jnp.float32), axis=1, keepdims=True)
    k = lax.broadcasted_iota(jnp.int32, (clusters, clusters), 0)
    m = lax.broadcasted_iota(jnp.int32, (clusters, clusters), 1)
    j = k % CL_DEV
    plus = (j == 1) & (m == k - 1)
    minus = ((j == 2) & ((m == k) | (m == k + 1))) | ((j == 3) & (m == k))
    mix = (jnp.where(plus, 1.0, 0.0) - jnp.where(minus, 1.0, 0.0)).astype(jnp.bfloat16)
    spread = jnp.broadcast_to(count, (clusters, 128)).astype(jnp.bfloat16)
    base = dot(mix, spread, NN)[:, :1]
    jcol = lax.broadcasted_iota(jnp.int32, (clusters, 1), 0) % CL_DEV
    base = base + jnp.where(jcol >= 2, float(PARTS * cap), 0.0)
    position = []
    for i, start in enumerate(range(0, rows, step)):
        piece = onehot[:, start : start + step].astype(jnp.float32)
        position.append(jnp.sum(piece * (ranks[i] + base), axis=0, keepdims=True))
    return jnp.concatenate(position, axis=1).astype(jnp.int32)


def first_kernel(devices, cap, steps, offsets):
    seg = PARTS * cap
    wide = lanes(seg)

    def kernel(ids_hbm, cover_hbm, emb_ref, unit_ref, where_hbm, meta_hbm, *rest):
        count = len(offsets)
        outs, scratch = rest[:count], rest[count:]
        ids_ref, cover_ref, raw_ref, rows_ref, where_ref, meta_ref, piece_ref = scratch[:7]
        in_sems, rows_sems, out_sems, small_sems = scratch[7:]
        me = lax.axis_index("clus")
        block = raw_ref.shape[0] // steps

        def load(i):
            part = pl.ds(i * block, block)
            return pltpu.make_async_copy(emb_ref.at[part], raw_ref.at[part], in_sems.at[i])

        def store(i):
            part = pl.ds(i * block, block)
            return pltpu.make_async_copy(rows_ref.at[part], unit_ref.at[part], rows_sems.at[i])

        small = [
            pltpu.make_async_copy(ids_hbm, ids_ref, small_sems.at[0]),
            pltpu.make_async_copy(cover_hbm, cover_ref, small_sems.at[1]),
            pltpu.make_async_copy(where_ref, where_hbm, small_sems.at[2]),
            pltpu.make_async_copy(meta_ref, meta_hbm, small_sems.at[3]),
        ]
        small[0].start()
        small[1].start()
        for i in range(steps):
            load(i).start(priority=i % 2)
        small[0].wait()
        small[1].wait()
        ids = ids_ref[...]
        owner = ids // CL_DEV
        position = place(ids, devices, cap)
        code = owner * seg + position
        where_ref[0:1, :] = code
        where_ref[1:2, :] = owner
        where_ref[2:3, :] = position
        own = hot(owner, devices)
        there = hot(position, wide)
        cover = cover_ref[...].astype(jnp.float32)
        cover = jnp.concatenate([cover[i : i + 1] for i in range(cover.shape[0])], axis=1)
        which = (ids - owner * CL_DEV).astype(jnp.float32)
        both = [own * cover.astype(jnp.bfloat16), own * which.astype(jnp.bfloat16)]
        both = dot(jnp.concatenate(both, axis=0), there, NT)
        meta_ref[:, 0, :wide] = both[:devices]
        meta_ref[:, 0, wide:] = both[devices:]
        small[2].start()
        small[3].start()
        picks = [hot(code, seg, (me ^ k) * seg) for k in offsets]
        found = [jnp.zeros((seg, rows_ref.shape[1]), jnp.float32) for _ in offsets]
        for i in range(steps):
            load(i).wait()
            if i == steps - 1:
                for before in range(steps - 1):
                    store(before).start(priority=before % 2)
            raw = raw_ref[i * block : (i + 1) * block, :]
            sums = jnp.sum(raw * raw, axis=-1, keepdims=True)
            unit = (raw * lax.rsqrt(sums + 1e-06)).astype(jnp.bfloat16)
            rows_ref[i * block : (i + 1) * block, :] = unit
            for j, pick in enumerate(picks):
                found[j] = found[j] + dot(pick[:, i * block : (i + 1) * block], unit, NN)
        store(steps - 1).start()
        send_pieces(found, meta_ref, seg, me, offsets, outs, piece_ref, out_sems)
        small[2].wait()
        small[3].wait()
        for i in range(steps):
            store(i).wait()

    return kernel


def send_pieces(found, meta_ref, seg, me, offsets, outs, piece_ref, sems):
    copies = []
    slabs = (piece_ref.shape[1] - TAIL) // seg
    index = lax.broadcasted_iota(jnp.int32, (TAIL, 128), 0)
    for i, (k, out_ref) in enumerate(zip(offsets, outs)):
        rows = found[i] if isinstance(found, list) else found(k)
        rows = rows.astype(jnp.bfloat16)
        for f in range(slabs):
            piece_ref[i, f * seg : (f + 1) * seg, :] = rows[:, f * 128 : (f + 1) * 128]
        row = meta_ref[me ^ k]
        tail = jnp.zeros((TAIL, 128), jnp.float32)
        for j in range(row.shape[1] // 128):
            tail = jnp.where(index == j, row[:, j * 128 : (j + 1) * 128], tail)
        piece_ref[i, slabs * seg :, :] = tail.astype(jnp.bfloat16)
        copies.append(pltpu.make_async_copy(piece_ref.at[i], out_ref, sems.at[i]))
        copies[-1].start()
    for copy in copies:
        copy.wait()


def rest_kernel(devices, cap, offsets):
    seg = PARTS * cap

    def kernel(where_ref, meta_ref, unit_ref, *rest):
        outs, (piece_ref, sems) = rest[: len(offsets)], rest[len(offsets) :]
        me = lax.axis_index("clus")

        def found(k):
            return dot(hot(where_ref[0:1, :], seg, (me ^ k) * seg), unit_ref[...], NN)

        send_pieces(found, meta_ref, seg, me, offsets, outs, piece_ref, sems)

    return kernel


def column(row):
    return jnp.transpose(jnp.broadcast_to(row, (128, row.shape[1])))


def pad_rows(piece, count):
    if piece.shape[0] == count:
        return piece
    fill = jnp.zeros((count - piece.shape[0], piece.shape[1]), piece.dtype)
    return jnp.concatenate([piece, fill], axis=0)


def repeat(col, n):
    return jnp.concatenate([col] * (n // 128), axis=1)


def gram_kernel(devices, cap, offsets, stops, which_stop):
    seg = PARTS * cap
    wide = lanes(seg)
    per_tile = max(1, 768 // cap)
    done = stops[which_stop - 1] if which_stop else 0
    new = stops[which_stop]
    xs = list(range(done, new))
    m = len(xs)
    meets = ((0, 1), (0, 1, 2), (1, 2))
    final = new == devices

    def kernel(*refs):
        pieces, refs = refs[:new], refs[new:]
        old_cols, refs = refs[:which_stop], refs[which_stop:]
        if which_stop:
            gains_ref, refs = refs[0], refs[1:]
        out_ref = refs[0]
        slabs = (pieces[0].shape[0] - TAIL) // seg

        def chunk(p, c):
            rows = [pieces[p][f * seg + c * cap : f * seg + (c + 1) * cap, :] for f in range(slabs)]
            return jnp.concatenate(rows, axis=1)

        def meta_of(p):
            tail = pieces[p][slabs * seg :, :].astype(jnp.float32)
            parts = [tail[j : j + 1] for j in range(2 * wide // 128)]
            half = len(parts) // 2
            return jnp.concatenate(parts[:half], axis=1), jnp.concatenate(parts[half:], axis=1)

        metas = [meta_of(p) for p in xs]
        right, right_cover, right_which, down = [], [], [], []
        for meet in meets:
            n = lanes(len(meet) * m * cap)
            fill = [jnp.full((1, n - len(meet) * m * cap), -1.0, jnp.float32)]
            fill = fill if fill[0].shape[1] else []
            right.append(pad_rows(jnp.concatenate([chunk(p, c) for c in meet for p in xs], axis=0), n))
            rows = [[meta[v][:, c * cap : (c + 1) * cap] for c in meet for meta in metas] for v in (0, 1)]
            right_cover.append(jnp.concatenate(rows[0] + fill, axis=1))
            right_which.append(jnp.concatenate(rows[1] + fill, axis=1))
            down.append(jnp.zeros((8, n), jnp.float32))
        cover_cols, which_cols = {}, {}
        first = 0
        for g in range(which_stop):
            for p in range(first, stops[g]):
                part = slice((p - first) * seg, (p - first + 1) * seg)
                cover_cols[p] = old_cols[g][part, :128]
                which_cols[p] = old_cols[g][part, 128:]
            first = stops[g]
        for i, p in enumerate(xs):
            cover_cols[p] = column(metas[i][0])[:seg]
            which_cols[p] = column(metas[i][1])[:seg]
            if not final:
                refs[1][i * seg : (i + 1) * seg, :128] = cover_cols[p]
                refs[1][i * seg : (i + 1) * seg, 128:] = which_cols[p]
        total, found = {}, {}
        for start in range(0, new, per_tile):
            members = range(start, min(start + per_tile, new))
            old = [p for p in members if p < done]
            for c, meet in enumerate(meets):
                n = right[c].shape[0]
                part = slice(c * cap, (c + 1) * cap)
                left = jnp.concatenate([chunk(p, c) for p in members], axis=0)
                similar = dot(left, right[c], NT)
                which = jnp.concatenate([which_cols[p][part] for p in members], axis=0)
                cover = jnp.concatenate([cover_cols[p][part] for p in members], axis=0)
                similar = jnp.where(repeat(which, n) == right_which[c], similar, -1e30)
                gain = jnp.maximum(similar - repeat(cover, n), 0.0)
                down[c] = down[c] + jnp.sum(gain.reshape(left.shape[0] // 8, 8, n), axis=0)
                if not old:
                    continue
                other = jnp.maximum(similar[: len(old) * cap] - right_cover[c], 0.0)
                folded = other[:, :128]
                for begin in range(128, n, 128):
                    folded = folded + other[:, begin : begin + 128]
                for i, p in enumerate(old):
                    found[p, c] = folded[i * cap : (i + 1) * cap]
        for p in range(done):
            mine = pad_rows(jnp.concatenate([found[p, c] for c in range(PARTS)], axis=0), wide)
            total[p] = jnp.sum(jnp.transpose(mine), axis=0, keepdims=True)
        down = [jnp.sum(d, axis=0, keepdims=True) for d in down]
        for i, p in enumerate(xs):
            values = []
            for c in range(PARTS):
                value = jnp.zeros((1, cap), jnp.float32)
                for d, meet in zip(down, meets):
                    if c in meet:
                        begin = (meet.index(c) * m + i) * cap
                        value = value + d[:, begin : begin + cap]
                values.append(value)
            if wide > seg:
                values.append(jnp.zeros((1, wide - seg), jnp.float32))
            total[p] = jnp.concatenate(values, axis=1)
        me = lax.axis_index("clus")
        for p in range(new):
            value = total[p]
            if p < done:
                value = value + gains_ref[p]
            if final:
                out_ref[me ^ offsets[p]] = value
            else:
                out_ref[p] = value

    return kernel


def last_kernel(kernel_devices):
    def kernel(where_ref, gains_ref, out_ref):
        gains = gains_ref[:, 0, :]
        high = gains.astype(jnp.bfloat16)
        rest = gains - high.astype(jnp.float32)
        mid = rest.astype(jnp.bfloat16)
        low = (rest - mid.astype(jnp.float32)).astype(jnp.bfloat16)
        there = hot(where_ref[2:3, :], gains.shape[1])
        parts = dot(jnp.concatenate([high, mid, low], axis=0), there, NN)
        count = gains.shape[0]
        found = parts[:count] + parts[count : 2 * count] + parts[2 * count :]
        index = lax.broadcasted_iota(jnp.int32, found.shape, 0)
        mine = jnp.where(index == where_ref[1:2, :], found, 0.0)
        out_ref[...] = jnp.sum(mine, axis=0, keepdims=True)

    return kernel


def call(kernel, outs, cost, name, vmem=24, **extra):
    return pl.pallas_call(
        kernel,
        out_shape=outs,
        compiler_params=pltpu.CompilerParams(vmem_limit_bytes=vmem * MIB),
        cost_estimate=pl.CostEstimate(flops=cost[0], bytes_accessed=cost[1], transcendentals=0),
        name=name,
        **extra,
    )


def sequence(devices):
    half = devices // 2
    quarter = max(1, half // 2)
    far = []
    for i in range(quarter):
        far += [half + i, half + quarter + i]
    near = sorted(range(1, half), key=lambda k: (-k.bit_length(), k))
    order = [0, far[0]]
    for i in range(half - 2):
        order += [far[i + 1], near[i]]
    return order + [near[-1], far[-1]]


def body(embeddings, coverage, cluster_ids):
    devices = lax.axis_size("clus")
    rows, width = embeddings.shape
    cap = 2 * rows // (CL_DEV * devices)
    seg = PARTS * cap
    wide = lanes(seg)
    offsets = sequence(devices)
    f32, bf16 = jnp.float32, jnp.bfloat16
    S = jax.ShapeDtypeStruct
    ids = cluster_ids.reshape(1, rows)
    cover = coverage.reshape(rows // 128, 128)
    unitg = devices // 16
    early = EARLY * unitg
    depth = DEPTH * unitg
    tall = width // 128 * seg + TAIL
    piece = S((tall, 128), bf16)

    def pieces_of(count):
        return dict(
            out_specs=[pl.BlockSpec(memory_space=pltpu.HBM)] * count,
            scratch_shapes=[pltpu.VMEM((count, tall, 128), bf16), pltpu.SemaphoreType.DMA((count,))],
        )

    full = pl.BlockSpec(memory_space=pltpu.VMEM)
    hbm = pl.BlockSpec(memory_space=pltpu.HBM)
    steps = 4
    lead = pieces_of(early)
    unit, where, meta, *sent = call(
        first_kernel(devices, cap, steps, offsets[1 : 1 + early]),
        [S((rows, width), bf16), S((3, rows), jnp.int32), S((devices, 1, 2 * wide), f32)] + [piece] * early,
        (2 * early * seg * rows * width, 4 * rows * width),
        "first",
        in_specs=[hbm] * 3,
        out_specs=[hbm] * 3 + lead["out_specs"],
        scratch_shapes=[pltpu.VMEM((1, rows), jnp.int32), pltpu.VMEM((rows // 128, 128), bf16)]
        + [pltpu.VMEM((rows, width), f32), pltpu.VMEM((rows, width), bf16)]
        + [pltpu.VMEM((3, rows), jnp.int32), pltpu.VMEM((devices, 1, 2 * wide), f32)]
        + [lead["scratch_shapes"][0]]
        + [pltpu.SemaphoreType.DMA((steps,))] * 2
        + [lead["scratch_shapes"][1], pltpu.SemaphoreType.DMA((4,))],
        vmem=56,
    )(ids, cover, embeddings)
    for name, ks in (("second", offsets[1 + early : 1 + depth]), ("rest", offsets[1 + depth :] + [0])):
        sent += call(
            rest_kernel(devices, cap, ks),
            [piece] * len(ks),
            (0, 0),
            name,
            in_specs=[full] * 3,
            vmem=20,
            **pieces_of(len(ks)),
        )(where, meta, unit)
    own = sent.pop()

    got = []
    for i, x in enumerate(sent):
        if i >= depth:
            x, got[i - depth] = lax.optimization_barrier((x, got[i - depth]))
        got.append(lax.ppermute(x, "clus", [(d, d ^ offsets[1 + i]) for d in range(devices)]))
    pieces = [own] + got

    gain_shape = S((devices, 1, wide), f32)
    stops = [stop * unitg for stop in STOPS]
    cols, gains = [], []
    for g, new in enumerate(stops):
        fresh = new - (stops[g - 1] if g else 0)
        gains, *more = call(
            gram_kernel(devices, cap, offsets, stops, g),
            [gain_shape] + [S((fresh * seg, 256), f32)] * (new < devices),
            (2 * new * seg * fresh * seg * width, 2 * new * seg * width),
            "gram",
            vmem=16,
        )(*pieces[:new], *cols, *([gains] if g else []))
        cols += more
    back = lax.all_to_all(gains, "clus", 0, 0, tiled=True)
    out = call(last_kernel(devices), S((1, rows), f32), (2 * rows * wide * 48, 8 * rows), "last")(where, back)
    return out.reshape(rows)


def solution(mesh):
    placed = (P(("parts", "clus"), None), P(("parts", "clus")), P(("parts", "clus"), None))
    return jax.shard_map(
        body, mesh=mesh, in_specs=placed, out_specs=P(("parts", "clus")), check_vma=False
    )
```

```python
import jax
import jax.numpy as jnp
from jax import lax
from jax.experimental import pallas as pl
from jax.experimental.pallas import tpu as pltpu
from jax.sharding import PartitionSpec as P

CL_DEV = 4
PARTS = 3
TAIL = 16
EARLY = 1
DEPTH = 4
STOPS = (4, 6, 8, 10, 12, 14, 15, 16)
MIB = 1024 * 1024

NN = (((1,), (0,)), ((), ()))
NT = (((1,), (1,)), ((), ()))


def dot(left, right, dims):
    return lax.dot_general(left, right, dims, preferred_element_type=jnp.float32)


def lanes(n):
    return -(-n // 128) * 128


def hot(values, count, first=0):
    index = lax.broadcasted_iota(jnp.int32, (count, values.shape[1]), 0) + first
    return jnp.where(index == values, 1.0, 0.0).astype(jnp.bfloat16)


def place(ids, devices, cap):
    rows = ids.shape[1]
    clusters = CL_DEV * devices
    step = 256
    onehot = hot(ids, clusters)
    before = lax.broadcasted_iota(jnp.int32, (step, step), 0) < lax.broadcasted_iota(
        jnp.int32, (step, step), 1
    )
    before = jnp.where(before, 1.0, 0.0).astype(jnp.bfloat16)
    count = jnp.zeros((clusters, 1), jnp.float32)
    ranks = []
    for start in range(0, rows, step):
        piece = onehot[:, start : start + step]
        ranks.append(dot(piece, before, NN) + count)
        count = count + jnp.sum(piece.astype(jnp.float32), axis=1, keepdims=True)
    k = lax.broadcasted_iota(jnp.int32, (clusters, clusters), 0)
    m = lax.broadcasted_iota(jnp.int32, (clusters, clusters), 1)
    j = k % CL_DEV
    plus = (j == 1) & (m == k - 1)
    minus = ((j == 2) & ((m == k) | (m == k + 1))) | ((j == 3) & (m == k))
    mix = (jnp.where(plus, 1.0, 0.0) - jnp.where(minus, 1.0, 0.0)).astype(jnp.bfloat16)
    spread = jnp.broadcast_to(count, (clusters, 128)).astype(jnp.bfloat16)
    base = dot(mix, spread, NN)[:, :1]
    jcol = lax.broadcasted_iota(jnp.int32, (clusters, 1), 0) % CL_DEV
    base = base + jnp.where(jcol >= 2, float(PARTS * cap), 0.0)
    position = []
    for i, start in enumerate(range(0, rows, step)):
        piece = onehot[:, start : start + step].astype(jnp.float32)
        position.append(jnp.sum(piece * (ranks[i] + base), axis=0, keepdims=True))
    return jnp.concatenate(position, axis=1).astype(jnp.int32)


def first_kernel(devices, cap, steps, offsets):
    seg = PARTS * cap
    wide = lanes(seg)

    def kernel(ids_hbm, cover_hbm, emb_ref, unit_ref, where_hbm, meta_hbm, *rest):
        count = len(offsets)
        outs, scratch = rest[:count], rest[count:]
        ids_ref, cover_ref, raw_ref, rows_ref, where_ref, meta_ref, piece_ref = scratch[:7]
        in_sems, rows_sems, out_sems, small_sems = scratch[7:]
        me = lax.axis_index("clus")
        block = raw_ref.shape[0] // steps

        def load(i):
            part = pl.ds(i * block, block)
            return pltpu.make_async_copy(emb_ref.at[part], raw_ref.at[part], in_sems.at[i])

        def store(i):
            part = pl.ds(i * block, block)
            return pltpu.make_async_copy(rows_ref.at[part], unit_ref.at[part], rows_sems.at[i])

        small = [
            pltpu.make_async_copy(ids_hbm, ids_ref, small_sems.at[0]),
            pltpu.make_async_copy(cover_hbm, cover_ref, small_sems.at[1]),
            pltpu.make_async_copy(where_ref, where_hbm, small_sems.at[2]),
            pltpu.make_async_copy(meta_ref, meta_hbm, small_sems.at[3]),
        ]
        small[0].start()
        small[1].start()
        for i in range(steps):
            load(i).start(priority=i % 2)
        small[0].wait()
        small[1].wait()
        ids = ids_ref[...]
        owner = ids // CL_DEV
        position = place(ids, devices, cap)
        code = owner * seg + position
        where_ref[0:1, :] = code
        where_ref[1:2, :] = owner
        where_ref[2:3, :] = position
        own = hot(owner, devices)
        there = hot(position, wide)
        cover = cover_ref[...].astype(jnp.float32)
        cover = jnp.concatenate([cover[i : i + 1] for i in range(cover.shape[0])], axis=1)
        which = (ids - owner * CL_DEV).astype(jnp.float32)
        both = [own * cover.astype(jnp.bfloat16), own * which.astype(jnp.bfloat16)]
        both = dot(jnp.concatenate(both, axis=0), there, NT)
        meta_ref[:, 0, :wide] = both[:devices]
        meta_ref[:, 0, wide:] = both[devices:]
        small[2].start()
        small[3].start()
        for i in range(steps):
            load(i).wait()
            if i == steps - 1:
                for before in range(steps - 1):
                    store(before).start(priority=before % 2)
            raw = raw_ref[i * block : (i + 1) * block, :]
            sums = jnp.sum(raw * raw, axis=-1, keepdims=True)
            unit = (raw * lax.rsqrt(sums + 1e-06)).astype(jnp.bfloat16)
            rows_ref[i * block : (i + 1) * block, :] = unit
        store(steps - 1).start()

        def found(k):
            return dot(hot(code, seg, (me ^ k) * seg), rows_ref[...], NN)

        send_pieces(found, meta_ref, seg, me, offsets, outs, piece_ref, out_sems)
        small[2].wait()
        small[3].wait()
        for i in range(steps):
            store(i).wait()

    return kernel


def send_pieces(found, meta_ref, seg, me, offsets, outs, piece_ref, sems):
    copies = []
    slabs = (piece_ref.shape[1] - TAIL) // seg
    index = lax.broadcasted_iota(jnp.int32, (TAIL, 128), 0)
    for i, (k, out_ref) in enumerate(zip(offsets, outs)):
        rows = found(k).astype(jnp.bfloat16)
        for f in range(slabs):
            piece_ref[i, f * seg : (f + 1) * seg, :] = rows[:, f * 128 : (f + 1) * 128]
        row = meta_ref[me ^ k]
        tail = jnp.zeros((TAIL, 128), jnp.float32)
        for j in range(row.shape[1] // 128):
            tail = jnp.where(index == j, row[:, j * 128 : (j + 1) * 128], tail)
        piece_ref[i, slabs * seg :, :] = tail.astype(jnp.bfloat16)
        copies.append(pltpu.make_async_copy(piece_ref.at[i], out_ref, sems.at[i]))
        copies[-1].start()
    for copy in copies:
        copy.wait()


def rest_kernel(devices, cap, offsets):
    seg = PARTS * cap

    def kernel(where_ref, meta_ref, unit_ref, *rest):
        outs, (piece_ref, sems) = rest[: len(offsets)], rest[len(offsets) :]
        me = lax.axis_index("clus")

        def found(k):
            return dot(hot(where_ref[0:1, :], seg, (me ^ k) * seg), unit_ref[...], NN)

        send_pieces(found, meta_ref, seg, me, offsets, outs, piece_ref, sems)

    return kernel


def column(row):
    return jnp.transpose(jnp.broadcast_to(row, (128, row.shape[1])))


def pad_rows(piece, count):
    if piece.shape[0] == count:
        return piece
    fill = jnp.zeros((count - piece.shape[0], piece.shape[1]), piece.dtype)
    return jnp.concatenate([piece, fill], axis=0)


def repeat(col, n):
    return jnp.concatenate([col] * (n // 128), axis=1)


def gram_kernel(devices, cap, offsets, stops, which_stop):
    seg = PARTS * cap
    wide = lanes(seg)
    per_tile = max(1, 768 // cap)
    done = stops[which_stop - 1] if which_stop else 0
    new = stops[which_stop]
    xs = list(range(done, new))
    m = len(xs)
    meets = ((0, 1), (0, 1, 2), (1, 2))
    final = new == devices

    def kernel(*refs):
        pieces, refs = refs[:new], refs[new:]
        old_cols, refs = refs[:which_stop], refs[which_stop:]
        if which_stop:
            gains_ref, refs = refs[0], refs[1:]
        out_ref = refs[0]
        slabs = (pieces[0].shape[0] - TAIL) // seg

        def chunk(p, c):
            rows = [pieces[p][f * seg + c * cap : f * seg + (c + 1) * cap, :] for f in range(slabs)]
            return jnp.concatenate(rows, axis=1)

        def meta_of(p):
            tail = pieces[p][slabs * seg :, :].astype(jnp.float32)
            parts = [tail[j : j + 1] for j in range(2 * wide // 128)]
            half = len(parts) // 2
            return jnp.concatenate(parts[:half], axis=1), jnp.concatenate(parts[half:], axis=1)

        metas = [meta_of(p) for p in xs]
        right, right_cover, right_which, down = [], [], [], []
        for meet in meets:
            n = lanes(len(meet) * m * cap)
            fill = [jnp.full((1, n - len(meet) * m * cap), -1.0, jnp.float32)]
            fill = fill if fill[0].shape[1] else []
            right.append(pad_rows(jnp.concatenate([chunk(p, c) for c in meet for p in xs], axis=0), n))
            rows = [[meta[v][:, c * cap : (c + 1) * cap] for c in meet for meta in metas] for v in (0, 1)]
            right_cover.append(jnp.concatenate(rows[0] + fill, axis=1))
            right_which.append(jnp.concatenate(rows[1] + fill, axis=1))
            down.append(jnp.zeros((8, n), jnp.float32))
        cover_cols, which_cols = {}, {}
        first = 0
        for g in range(which_stop):
            for p in range(first, stops[g]):
                part = slice((p - first) * seg, (p - first + 1) * seg)
                cover_cols[p] = old_cols[g][part, :128]
                which_cols[p] = old_cols[g][part, 128:]
            first = stops[g]
        for i, p in enumerate(xs):
            cover_cols[p] = column(metas[i][0])[:seg]
            which_cols[p] = column(metas[i][1])[:seg]
            if not final:
                refs[1][i * seg : (i + 1) * seg, :128] = cover_cols[p]
                refs[1][i * seg : (i + 1) * seg, 128:] = which_cols[p]
        total, found = {}, {}
        for start in range(0, new, per_tile):
            members = range(start, min(start + per_tile, new))
            old = [p for p in members if p < done]
            for c, meet in enumerate(meets):
                n = right[c].shape[0]
                part = slice(c * cap, (c + 1) * cap)
                left = jnp.concatenate([chunk(p, c) for p in members], axis=0)
                similar = dot(left, right[c], NT)
                which = jnp.concatenate([which_cols[p][part] for p in members], axis=0)
                cover = jnp.concatenate([cover_cols[p][part] for p in members], axis=0)
                similar = jnp.where(repeat(which, n) == right_which[c], similar, -1e30)
                gain = jnp.maximum(similar - repeat(cover, n), 0.0)
                down[c] = down[c] + jnp.sum(gain.reshape(left.shape[0] // 8, 8, n), axis=0)
                if not old:
                    continue
                other = jnp.maximum(similar[: len(old) * cap] - right_cover[c], 0.0)
                folded = other[:, :128]
                for begin in range(128, n, 128):
                    folded = folded + other[:, begin : begin + 128]
                for i, p in enumerate(old):
                    found[p, c] = folded[i * cap : (i + 1) * cap]
        for p in range(done):
            mine = pad_rows(jnp.concatenate([found[p, c] for c in range(PARTS)], axis=0), wide)
            total[p] = jnp.sum(jnp.transpose(mine), axis=0, keepdims=True)
        down = [jnp.sum(d, axis=0, keepdims=True) for d in down]
        for i, p in enumerate(xs):
            values = []
            for c in range(PARTS):
                value = jnp.zeros((1, cap), jnp.float32)
                for d, meet in zip(down, meets):
                    if c in meet:
                        begin = (meet.index(c) * m + i) * cap
                        value = value + d[:, begin : begin + cap]
                values.append(value)
            if wide > seg:
                values.append(jnp.zeros((1, wide - seg), jnp.float32))
            total[p] = jnp.concatenate(values, axis=1)
        me = lax.axis_index("clus")
        for p in range(new):
            value = total[p]
            if p < done:
                value = value + gains_ref[p]
            if final:
                out_ref[me ^ offsets[p]] = value
            else:
                out_ref[p] = value

    return kernel


def last_kernel(kernel_devices):
    def kernel(where_ref, gains_ref, out_ref):
        gains = gains_ref[:, 0, :]
        high = gains.astype(jnp.bfloat16)
        rest = gains - high.astype(jnp.float32)
        mid = rest.astype(jnp.bfloat16)
        low = (rest - mid.astype(jnp.float32)).astype(jnp.bfloat16)
        there = hot(where_ref[2:3, :], gains.shape[1])
        parts = dot(jnp.concatenate([high, mid, low], axis=0), there, NN)
        count = gains.shape[0]
        found = parts[:count] + parts[count : 2 * count] + parts[2 * count :]
        index = lax.broadcasted_iota(jnp.int32, found.shape, 0)
        mine = jnp.where(index == where_ref[1:2, :], found, 0.0)
        out_ref[...] = jnp.sum(mine, axis=0, keepdims=True)

    return kernel


def call(kernel, outs, cost, name, vmem=24, **extra):
    return pl.pallas_call(
        kernel,
        out_shape=outs,
        compiler_params=pltpu.CompilerParams(vmem_limit_bytes=vmem * MIB),
        cost_estimate=pl.CostEstimate(flops=cost[0], bytes_accessed=cost[1], transcendentals=0),
        name=name,
        **extra,
    )


def sequence(devices):
    half = devices // 2
    quarter = max(1, half // 2)
    far = []
    for i in range(quarter):
        far += [half + i, half + quarter + i]
    near = sorted(range(1, half), key=lambda k: (-k.bit_length(), k))
    order = [0, far[0]]
    for i in range(half - 2):
        order += [far[i + 1], near[i]]
    return order + [near[-1], far[-1]]


def body(embeddings, coverage, cluster_ids):
    devices = lax.axis_size("clus")
    rows, width = embeddings.shape
    cap = 2 * rows // (CL_DEV * devices)
    seg = PARTS * cap
    wide = lanes(seg)
    offsets = sequence(devices)
    f32, bf16 = jnp.float32, jnp.bfloat16
    S = jax.ShapeDtypeStruct
    ids = cluster_ids.reshape(1, rows)
    cover = coverage.reshape(rows // 128, 128)
    unitg = devices // 16
    early = EARLY * unitg
    depth = DEPTH * unitg
    tall = width // 128 * seg + TAIL
    piece = S((tall, 128), bf16)

    def pieces_of(count):
        return dict(
            out_specs=[pl.BlockSpec(memory_space=pltpu.HBM)] * count,
            scratch_shapes=[pltpu.VMEM((count, tall, 128), bf16), pltpu.SemaphoreType.DMA((count,))],
        )

    full = pl.BlockSpec(memory_space=pltpu.VMEM)
    hbm = pl.BlockSpec(memory_space=pltpu.HBM)
    steps = 4
    lead = pieces_of(early)
    unit, where, meta, *sent = call(
        first_kernel(devices, cap, steps, offsets[1 : 1 + early]),
        [S((rows, width), bf16), S((3, rows), jnp.int32), S((devices, 1, 2 * wide), f32)] + [piece] * early,
        (2 * early * seg * rows * width, 4 * rows * width),
        "first",
        in_specs=[hbm] * 3,
        out_specs=[hbm] * 3 + lead["out_specs"],
        scratch_shapes=[pltpu.VMEM((1, rows), jnp.int32), pltpu.VMEM((rows // 128, 128), bf16)]
        + [pltpu.VMEM((rows, width), f32), pltpu.VMEM((rows, width), bf16)]
        + [pltpu.VMEM((3, rows), jnp.int32), pltpu.VMEM((devices, 1, 2 * wide), f32)]
        + [lead["scratch_shapes"][0]]
        + [pltpu.SemaphoreType.DMA((steps,))] * 2
        + [lead["scratch_shapes"][1], pltpu.SemaphoreType.DMA((4,))],
        vmem=56,
    )(ids, cover, embeddings)
    for name, ks in (("second", offsets[1 + early : 1 + depth]), ("rest", offsets[1 + depth :] + [0])):
        sent += call(
            rest_kernel(devices, cap, ks),
            [piece] * len(ks),
            (0, 0),
            name,
            in_specs=[full] * 3,
            vmem=20,
            **pieces_of(len(ks)),
        )(where, meta, unit)
    own = sent.pop()

    got = []
    for i, x in enumerate(sent):
        if i >= depth:
            x, got[i - depth] = lax.optimization_barrier((x, got[i - depth]))
        got.append(lax.ppermute(x, "clus", [(d, d ^ offsets[1 + i]) for d in range(devices)]))
    pieces = [own] + got

    gain_shape = S((devices, 1, wide), f32)
    stops = [stop * unitg for stop in STOPS]
    cols, gains = [], []
    for g, new in enumerate(stops):
        fresh = new - (stops[g - 1] if g else 0)
        gains, *more = call(
            gram_kernel(devices, cap, offsets, stops, g),
            [gain_shape] + [S((fresh * seg, 256), f32)] * (new < devices),
            (2 * new * seg * fresh * seg * width, 2 * new * seg * width),
            "gram",
            vmem=16,
        )(*pieces[:new], *cols, *([gains] if g else []))
        cols += more
    back = lax.all_to_all(gains, "clus", 0, 0, tiled=True)
    out = call(last_kernel(devices), S((1, rows), f32), (2 * rows * wide * 48, 8 * rows), "last")(where, back)
    return out.reshape(rows)


def solution(mesh):
    placed = (P(("parts", "clus"), None), P(("parts", "clus")), P(("parts", "clus"), None))
    return jax.shard_map(
        body, mesh=mesh, in_specs=placed, out_specs=P(("parts", "clus")), check_vma=False
    )
```
